32 devices in a mesh: ctx: 8 (over y, x, core), tp: 4 (over z).
Axes of the slice: x: 2, y: 2, z: 4, core: 2. Of those that a mesh axis runs over, the one named last changes fastest.
Arguments:
- out_grad: bfloat16 [2048, 8192], P(('ctx', 'tp')), may hold values from -6 to 6
- saved_input: bfloat16 [2048, 8192], P(('ctx', 'tp')), may hold values from -6 to 6
- explicit_filter_weights: float32 [128, 8192], P(None, 'tp'), may hold values from -0.5 to 0.5
- gate_taps: float32 [3, 8192], P(None, 'tp'), may hold values from -3.5 to 3.5
- value_featurizer_weights: float32 [3, 8192], P(None, 'tp'), may hold values from -3.5 to 3.5
Outputs:
- input_grad: bfloat16 [2048, 8192], P('ctx', 'tp')
- explicit_filter_gradient: float32 [128, 8192], P(None, 'tp')
- gate_grad: float32 [3, 8192], P(None, 'tp')
- value_grad: float32 [3, 8192], P(None, 'tp')
The draws below stay inside these ranges and needn't reach their ends.
All inputs are finite; a program needn't handle non-finite values.
Results may differ from the reference program's by a relative error of at most 0.004.
Values may be sent and summed in bfloat16 or wider, within the bound.
No kernel may reach another device: no remote copies, remote signals or barrier semaphores. Data moves between devices by JAX's collectives and lax.ppermute only.
A program may use at most 64 MiB of HBM per device.

```python
import jax
import jax.numpy as jnp
from jax import lax

D = 8192
FILTER_LENGTH = 128
FK = 3
TOKENS = 2048


def level_of(own_key, dims, shards, least, largest):
    level = 1.0
    for position, shards_of in shards:
        heights = jax.random.uniform(jax.random.fold_in(jax.random.fold_in(own_key, 6), position), (shards_of,), jnp.float32, least / len(shards), largest / len(shards))
        level = level * jnp.repeat(jnp.exp(heights), dims[position] // shards_of).reshape((-1,) + (1,) * (len(dims) - 1 - position))
    return level


def gaussian(key, extent, deviation, bound, pieces=(), kind=jnp.bfloat16):
    result = jax.random.normal(key, extent, jnp.float32) * deviation
    if len(pieces) > 0:
        result = level_of(key, extent, pieces, -0.22, 0.18) * result
    return jnp.clip(result, min=-bound, max=bound).astype(kind)


def setup_inputs(seed: int = 0) -> dict:
    arg_keys = jax.random.split(jax.random.key(seed), 6)
    out_grad = gaussian(arg_keys[0], (TOKENS, D), 1.0, 6.0, ((0, 32),))
    saved_input = gaussian(arg_keys[1], (TOKENS, D), 1.0, 6.0, ((0, 32),))
    explicit_filter_weights = gaussian(arg_keys[2], (FILTER_LENGTH, D), FILTER_LENGTH ** -0.5, 0.5, ((1, 4),), jnp.float32)
    gate_taps = gaussian(arg_keys[3], (FK, D), FK ** -0.5, 3.5, ((1, 4),), jnp.float32)
    value_featurizer_weights = gaussian(arg_keys[4], (FK, D), FK ** -0.5, 3.5, ((1, 4),), jnp.float32)
    return {"out_grad": out_grad, "saved_input": saved_input, "explicit_filter_weights": explicit_filter_weights, "gate_taps": gate_taps, "value_featurizer_weights": value_featurizer_weights}


def causal_mixing(padded, taps, count):
    filter_extent = taps.shape[0]
    total = taps[0] * padded[filter_extent - 1:filter_extent - 1 + count]
    for j in range(1, filter_extent):
        total = total + taps[j] * padded[filter_extent - 1 - j:filter_extent - 1 - j + count]
    return total


def anticausal(padded, taps, count):
    total = taps[0] * padded[0:count]
    for j in range(1, taps.shape[0]):
        total = total + taps[j] * padded[j:j + count]
    return total


def delayed_input(left, right, filter_extent, base):
    count = left.shape[0]
    return jnp.stack([jnp.sum(left * right[base - j:base - j + count], axis=0) for j in range(filter_extent)])


def compose(value_featurizer_weights, explicit_filter_weights):
    short = value_featurizer_weights.shape[0]
    filter_extent = explicit_filter_weights.shape[0]
    total = jnp.zeros((filter_extent + short - 1, explicit_filter_weights.shape[1]), jnp.float32)
    for i in range(short):
        total = total.at[i:i + filter_extent].add(value_featurizer_weights[i] * explicit_filter_weights)
    return total


def channel_block(args):
    out_grad, saved_input, explicit_filter_weights, gate_taps, value_featurizer_weights = args
    sequence_length = out_grad.shape[0]
    width = out_grad.shape[1]
    reach = FILTER_LENGTH + FK - 2
    extended_input = jnp.concatenate([jnp.zeros((reach, width), jnp.float32), saved_input.astype(jnp.float32)])
    extended_value = causal_mixing(extended_input, value_featurizer_weights, sequence_length + FILTER_LENGTH - 1)
    qext = causal_mixing(extended_input, gate_taps, sequence_length + FILTER_LENGTH - 1)
    gate = qext[FILTER_LENGTH - 1:]
    pext = causal_mixing(extended_input, explicit_filter_weights, sequence_length + FK - 1)
    mixed_signal = causal_mixing(extended_value, explicit_filter_weights, sequence_length)
    grad_f = out_grad.astype(jnp.float32)
    grad_q = grad_f * mixed_signal
    mixed_signal_gradient = grad_f * gate
    gradient_scale = jnp.float32(TOKENS ** -0.5)
    explicit_filter_gradient = delayed_input(mixed_signal_gradient, extended_value, FILTER_LENGTH, FILTER_LENGTH - 1) * gradient_scale
    gate_grad = delayed_input(grad_q, extended_input, FK, reach) * gradient_scale
    value_grad = delayed_input(mixed_signal_gradient, pext, FK, FK - 1) * gradient_scale
    combined = compose(value_featurizer_weights, explicit_filter_weights)
    zpad = jnp.concatenate([mixed_signal_gradient, jnp.zeros((reach, width), jnp.float32)])
    qpad = jnp.concatenate([grad_q, jnp.zeros((FK - 1, width), jnp.float32)])
    input_grad = anticausal(zpad, combined, sequence_length) + anticausal(qpad, gate_taps, sequence_length)
    return input_grad.astype(jnp.bfloat16), explicit_filter_gradient, gate_grad, value_grad


def reference(out_grad, saved_input, explicit_filter_weights, gate_taps, value_featurizer_weights):
    block = 512 if D % 512 == 0 else D
    count = D // block

    def split_cols(array):
        return array.reshape(array.shape[0], count, block).transpose(1, 0, 2)

    def join_cols(array):
        return array.transpose(1, 0, 2).reshape(array.shape[1], D)

    results = lax.map(channel_block, (split_cols(out_grad), split_cols(saved_input), split_cols(explicit_filter_weights), split_cols(gate_taps), split_cols(value_featurizer_weights)))
    return join_cols(results[0]), join_cols(results[1]), join_cols(results[2]), join_cols(results[3])
```

```python
import math

import jax
import jax.numpy as jnp
import numpy as np
from jax import lax
from jax.experimental import pallas as pl
from jax.experimental.pallas import tpu as pltpu
from jax.sharding import PartitionSpec as P

F32 = jnp.float32
BF16 = jnp.bfloat16


def halves(x):
    high = x.astype(BF16)
    return high, (x - high.astype(F32)).astype(BF16)


def stacked_rows(x):
    high, low = halves(x)
    return jnp.concatenate([high, high, low], axis=0)


def product(matrix, x):
    return jnp.dot(matrix, x, preferred_element_type=F32)


def transforms(extent):
    points = 2 * extent
    angle = np.pi * np.outer(2 * np.arange(extent) + 1, np.arange(points)) / points
    whole = np.concatenate([np.cos(angle), -np.sin(angle)])
    back = whole.T / extent
    back = np.concatenate([-back[extent:], back[:extent]])

    def split(matrix):
        high = matrix.astype(jnp.bfloat16)
        low = (matrix - high.astype(np.float64)).astype(jnp.bfloat16)
        return np.concatenate([high, low, high], axis=1)

    return split(whole), split(whole[:, :extent]), split(back)


def parts(x):
    half = x.shape[0] // 2
    return x[:half], x[half:]


def times(a, b):
    ar, ai = parts(a)
    br, bi = parts(b)
    return ar * br - ai * bi, ar * bi + ai * br


def times_conjugate(a, b):
    ar, ai = parts(a)
    br, bi = parts(b)
    return ar * br + ai * bi, ai * br - ar * bi


def joined(pair):
    return jnp.concatenate(pair, axis=0)


def delayed(x, by):
    return pltpu.roll(x, by, 0)


def advanced(x, by):
    return pltpu.roll(x, x.shape[0] - by, 0)


def signal_kernel(
    u_ref, halo_ref, h_ref, w_ref, forward_ref, short_ref, inverse_ref, v_ref, hs_ref, z_ref
):
    extent = h_ref.shape[0]
    rows = u_ref.shape[0]
    u = jnp.concatenate([halo_ref[...].astype(F32), u_ref[...].astype(F32)], axis=0)
    value = w_ref[0:1] * u
    for i in range(1, w_ref.shape[0]):
        value = value + w_ref[i : i + 1] * delayed(u, i)
    value = value[halo_ref.shape[0] - extent :]
    high, low = halves(value)
    spectrum_h = product(short_ref[...], stacked_rows(h_ref[...]))
    hs_ref[...] = spectrum_h
    for b in range(rows // extent):
        window = slice(b * extent, (b + 2) * extent)
        spectrum = product(
            forward_ref[...], jnp.concatenate([high[window], high[window], low[window]], axis=0)
        )
        v_ref[b] = spectrum
        z = product(inverse_ref[:extent], stacked_rows(joined(times(spectrum, spectrum_h))))
        z_ref[b * extent : (b + 1) * extent] = -z


def gradient_kernel(
    scale,
    pieces,
    me_ref,
    *refs,
):
    g_refs = refs[:pieces]
    (
        u_ref,
        halo_ref,
        v_ref,
        hs_ref,
        z_ref,
        gate_ref,
        w_ref,
        short_ref,
        inverse_ref,
        grad_ref,
        head_ref,
        sums_ref,
        g_all,
    ) = refs[pieces:]
    extent = hs_ref.shape[0] // 2
    rows, width = u_ref.shape
    lead = halo_ref.shape[0]
    taps = gate_ref.shape[0]
    piece = g_refs[0].shape[0]
    for k in range(pieces):
        source = lax.rem(me_ref[0] + (pieces - k), pieces)
        start = pl.multiple_of(source * piece, piece)
        g_all[pl.ds(start, piece), :] = g_refs[k][...].astype(F32)
    g = g_all[...]
    u = jnp.concatenate([halo_ref[...].astype(F32), u_ref[...].astype(F32)], axis=0)
    late = [u] + [delayed(u, i) for i in range(1, taps)]
    q = gate_ref[0:1] * late[0][lead:]
    for i in range(1, taps):
        q = q + gate_ref[i : i + 1] * late[i][lead:]
    dz = g * q
    dq = g * z_ref[...]
    spectrum_h = hs_ref[...]
    correlation = None
    blocks = rows // extent
    back = [jnp.zeros((lead - extent, width), F32)]
    carried = None
    for b in range(blocks):
        spectrum = product(short_ref[...], stacked_rows(dz[b * extent : (b + 1) * extent]))
        term = times_conjugate(spectrum, v_ref[b])
        correlation = (
            term if correlation is None else tuple(x + y for x, y in zip(correlation, term))
        )
        both = product(
            inverse_ref[...], stacked_rows(joined(times_conjugate(spectrum, spectrum_h)))
        )
        back.append(both[:extent] if carried is None else both[:extent] + carried)
        carried = both[extent:]
    back.append(carried)
    r = jnp.concatenate(back, axis=0)
    lags = product(inverse_ref[:extent], stacked_rows(joined(correlation)))
    sums_ref[0:extent] = lags * scale
    rest = [jnp.sum(dq * late[i][lead:], axis=0, keepdims=True) for i in range(taps)]
    rest += [jnp.sum(r * late[i], axis=0, keepdims=True) for i in range(taps)]
    spare = sums_ref.shape[0] - extent - 2 * taps
    rest.append(jnp.zeros((spare, width), F32))
    sums_ref[extent:] = jnp.concatenate(rest, axis=0) * scale
    padded = jnp.concatenate([jnp.zeros((lead, width), F32), dq], axis=0)
    total = w_ref[0:1] * r + gate_ref[0:1] * padded
    for i in range(1, taps):
        total = total + advanced(w_ref[i : i + 1] * r + gate_ref[i : i + 1] * padded, i)
    head_ref[...] = total[:lead].astype(BF16)
    grad_ref[...] = total[lead:].astype(BF16)


def whole_block(shape):
    return pl.BlockSpec(shape, lambda j, *_: (0,) * len(shape))


def columns(shape):
    return pl.BlockSpec(shape, lambda j, *_: (0,) * (len(shape) - 1) + (j,))


VMEM_LIMIT = 48 * 1024 * 1024


def signal_step(u, halo, h, w, matrices, block):
    rows, width = u.shape
    extent = h.shape[0]
    forward, short, inverse = matrices
    blocks = rows // extent
    return pl.pallas_call(
        signal_kernel,
        grid=(width // block,),
        in_specs=[
            columns((rows, block)),
            columns((halo.shape[0], block)),
            columns((extent, block)),
            columns((w.shape[0], block)),
            whole_block(forward.shape),
            whole_block(short.shape),
            whole_block(inverse.shape),
        ],
        out_specs=[
            columns((blocks, 2 * extent, block)),
            columns((2 * extent, block)),
            columns((rows, block)),
        ],
        out_shape=[
            jax.ShapeDtypeStruct((blocks, 2 * extent, width), F32),
            jax.ShapeDtypeStruct((2 * extent, width), F32),
            jax.ShapeDtypeStruct((rows, width), F32),
        ],
        compiler_params=pltpu.CompilerParams(vmem_limit_bytes=VMEM_LIMIT),
        name="signal_step",
    )(u, halo, h, w, forward, short, inverse)


def gradient_step(g_pieces, me, u, halo, v, hs, z, gate, w, matrices, scale, block):
    rows, width = u.shape
    extent = hs.shape[0] // 2
    taps = gate.shape[0]
    lead = halo.shape[0]
    _, short, inverse = matrices
    blocks = rows // extent
    count = extent + -(-2 * taps // 8) * 8

    def kernel(*refs):
        gradient_kernel(scale, len(g_pieces), *refs)

    return pl.pallas_call(
        kernel,
        grid_spec=pltpu.PrefetchScalarGridSpec(
            num_scalar_prefetch=1,
            grid=(width // block,),
            in_specs=[columns((g.shape[0], block)) for g in g_pieces]
            + [
                columns((rows, block)),
                columns((lead, block)),
                columns((blocks, 2 * extent, block)),
                columns((2 * extent, block)),
                columns((rows, block)),
                columns((taps, block)),
                columns((taps, block)),
                whole_block(short.shape),
                whole_block(inverse.shape),
            ],
            out_specs=[
                columns((rows, block)),
                columns((lead, block)),
                columns((count, block)),
            ],
            scratch_shapes=[pltpu.VMEM((rows, block), F32)],
        ),
        out_shape=[
            jax.ShapeDtypeStruct((rows, width), BF16),
            jax.ShapeDtypeStruct((lead, width), BF16),
            jax.ShapeDtypeStruct((count, width), F32),
        ],
        compiler_params=pltpu.CompilerParams(vmem_limit_bytes=VMEM_LIMIT),
        name="gradient_step",
    )(me, *g_pieces, u, halo, v, hs, z, gate, w, short, inverse)


def order_kernel(pieces, me_ref, *refs):
    out_ref, tail_ref = refs[pieces:]
    piece = refs[0].shape[0]
    for k in range(pieces):
        source = lax.rem(me_ref[0] + (pieces - k), pieces)
        start = pl.multiple_of(source * piece, piece)
        out_ref[pl.ds(start, piece), :] = refs[k][...]
    tail_ref[...] = out_ref[out_ref.shape[0] - tail_ref.shape[0] :]


def in_order(pieces, me, lead, block):
    piece, width = pieces[0].shape
    rows = piece * len(pieces)

    def kernel(*refs):
        order_kernel(len(pieces), *refs)

    return pl.pallas_call(
        kernel,
        grid_spec=pltpu.PrefetchScalarGridSpec(
            num_scalar_prefetch=1,
            grid=(width // block,),
            in_specs=[columns((piece, block)) for _ in pieces],
            out_specs=[columns((rows, block)), columns((lead, block))],
        ),
        out_shape=[
            jax.ShapeDtypeStruct((rows, width), BF16),
            jax.ShapeDtypeStruct((lead, width), BF16),
        ],
        name="token_order",
    )(me, *pieces)


def exchange(x, axis):
    count = lax.axis_size(axis)
    me = lax.axis_index(axis)
    width = x.shape[1] // count
    pieces = []
    for k in range(count):
        to = lax.rem(me + k, count)
        pieces.append(lax.dynamic_slice_in_dim(x, to * width, width, axis=1))
    got = [None] * count
    got[0] = pieces[0]
    for k in sorted(range(1, count), key=lambda k: abs(2 * k - count)):
        got[k] = lax.ppermute(pieces[k], axis, [(i, (i + k) % count) for i in range(count)])
    return got


def shifted(x, axis, by):
    count = lax.axis_size(axis)
    pairs = [(i, i + by) for i in range(count) if 0 <= i + by < count]
    return lax.ppermute(x, axis, pairs)


def partner(x, axis, bit):
    count = lax.axis_size(axis)
    return lax.ppermute(x, axis, [(i, i ^ bit) for i in range(count)])


def summed(x, axis):
    count = lax.axis_size(axis)
    me = lax.axis_index(axis)
    width = x.shape[1] // 2
    side = lax.rem(me, 2)
    own = lax.dynamic_slice_in_dim(x, side * width, width, axis=1)
    other = lax.dynamic_slice_in_dim(x, (1 - side) * width, width, axis=1)
    own = own + partner(other, axis, 1)
    bit = 2
    while bit < count:
        short = own.astype(BF16)
        own = short.astype(F32) + partner(short, axis, bit).astype(F32)
        bit *= 2
    other = partner(own, axis, 1)
    first = jnp.where(side == 0, own, other)
    second = jnp.where(side == 0, other, own)
    return jnp.concatenate([first, second], axis=1)


def shards(out_grad, saved_input, explicit_filter_weights, gate_taps, value_featurizer_weights):
    h, gate, w = explicit_filter_weights, gate_taps, value_featurizer_weights
    extent, taps = h.shape[0], gate.shape[0]
    me = lax.axis_index("tp").astype(jnp.int32).reshape(1)
    rows = out_grad.shape[0] * lax.axis_size("tp")
    lead = -(-(extent + taps - 2) // 16) * 16
    block = 256
    matrices = tuple(jnp.asarray(m) for m in transforms(extent))
    u_pieces = exchange(saved_input, "tp")
    g_pieces = exchange(out_grad, "tp")
    u, tail = in_order(u_pieces, me, lead, min(1024, h.shape[1]))
    halo = shifted(tail, "ctx", 1)
    v, hs, z = signal_step(u, halo, h, w, matrices, block)
    scale = 1.0 / math.sqrt(rows * lax.axis_size("ctx"))
    grad, head, sums = gradient_step(
        g_pieces, me, u, halo, v, hs, z, gate, w, matrices, scale, block
    )
    incoming = shifted(head, "ctx", -1)
    end = (grad[rows - lead :].astype(F32) + incoming.astype(F32)).astype(BF16)
    input_grad = jnp.concatenate([grad[: rows - lead], end])
    sums = summed(sums, "ctx")
    return (
        input_grad,
        sums[:extent],
        sums[extent : extent + taps],
        sums[extent + taps : extent + 2 * taps],
    )


def solution(mesh):
    placed = (
        P(("ctx", "tp"), None),
        P(("ctx", "tp"), None),
        P(None, "tp"),
        P(None, "tp"),
        P(None, "tp"),
    )
    return jax.shard_map(
        shards,
        mesh=mesh,
        in_specs=placed,
        out_specs=(P("ctx", "tp"), P(None, "tp"), P(None, "tp"), P(None, "tp")),
        check_vma=False,
    )
```

```python
import math

import jax
import jax.numpy as jnp
import numpy as np
from jax import lax
from jax.experimental import pallas as pl
from jax.experimental.pallas import tpu as pltpu
from jax.sharding import PartitionSpec as P

F32 = jnp.float32
BF16 = jnp.bfloat16
VMEM_LIMIT = 16 * 1024 * 1024
BLOCK = 1024
BRIEF = pl.CostEstimate(flops=1000, bytes_accessed=1000, transcendentals=0)
LONG = pl.CostEstimate(flops=20_000_000_000, bytes_accessed=100_000_000, transcendentals=0)


STRIP = 16


def strips(rows):
    return [slice(i, i + STRIP) for i in range(0, rows, STRIP)]


def put_halves(x, high_ref, low_ref, rows):
    high = x.astype(BF16)
    high_ref[rows] = high
    low_ref[rows] = (x - high.astype(F32)).astype(BF16)


def stacked_rows(high_ref, low_ref, rows=slice(None)):
    high = high_ref[rows]
    return jnp.concatenate([high, high, low_ref[rows]], axis=0)


def product(matrix, x):
    return jnp.dot(matrix, x, preferred_element_type=F32)


def transforms(extent):
    points = 2 * extent
    angle = np.pi * np.outer(2 * np.arange(extent) + 1, np.arange(points)) / points
    whole = np.concatenate([np.cos(angle), -np.sin(angle)])
    back = whole.T / extent

    def split(matrix, terms=3):
        high = matrix.astype(jnp.bfloat16)
        low = (matrix - high.astype(np.float64)).astype(jnp.bfloat16)
        return np.concatenate([high, low, high][:terms], axis=1)

    return {
        "both": split(whole, 2),
        "short": split(whole[:, :extent]),
        "inverse": split(np.concatenate([-back[extent:], back[:extent]])),
        "around": split(-back[extent - 8 :]),
    }


def delayed(before, x, by):
    return pltpu.roll(jnp.concatenate([before, x], axis=0), by, 0)[8:]


def advanced(x, after, by):
    both = jnp.concatenate([x, after], axis=0)
    return pltpu.roll(both, both.shape[0] - by, 0)[: x.shape[0]]


def folded(x):
    return sum(x[i : i + 8] for i in range(8, x.shape[0], 8)) + x[:8]


def filtered(u, before, taps):
    value = taps[0] * u
    for j in range(1, len(taps)):
        value = value + taps[j] * delayed(before, u, j)
    return value


def convolved(matrix, spectrum, hs_ref, high_ref, low_ref):
    for at in strips(hs_ref.shape[0] // 2):
        im = slice(at.start + hs_ref.shape[0] // 2, at.stop + hs_ref.shape[0] // 2)
        ur, ui, hr, hi = spectrum[at], spectrum[im], hs_ref[at], hs_ref[im]
        put_halves(ur * hr - ui * hi, high_ref, low_ref, at)
        put_halves(ur * hi + ui * hr, high_ref, low_ref, im)
    return product(matrix, stacked_rows(high_ref, low_ref))


def twice(x):
    return jnp.concatenate([x, x], axis=0)


def signal_kernel(
    u_ref, halo_ref, h_ref, w_ref, both_ref, short_ref, around_ref, us_ref, hs_ref, z_ref, *scratch
):
    high_h, low_h, high_p, low_p, p_ref = scratch
    extent = h_ref.shape[0]
    lead, width = halo_ref.shape
    blocks = us_ref.shape[0]
    for at in strips(extent):
        put_halves(-h_ref[at], high_h, low_h, at)
    hs_ref[...] = product(short_ref[...], stacked_rows(high_h, low_h))
    for b in range(blocks):
        last = u_ref[b * extent : (b + 1) * extent]
        first = halo_ref[lead - extent :] if b == 0 else u_ref[(b - 1) * extent : b * extent]
        us_ref[b] = product(both_ref[...], jnp.concatenate([first, last] * 2, axis=0))
    for b in range(blocks):
        matrix = around_ref[...] if b == 0 else around_ref[8:]
        rows = slice(0, extent + 8) if b == 0 else slice(8 + b * extent, 8 + (b + 1) * extent)
        p_ref[rows] = convolved(matrix, us_ref.at[b], hs_ref, high_p.at[b], low_p.at[b])
    ahead = halo_ref[lead - extent - STRIP : lead - extent].astype(F32)[STRIP - 1 :]
    final = u_ref[extent - STRIP : extent].astype(F32)[STRIP - 1 :]
    mend = h_ref[extent - 1 : extent] * (ahead + final)
    at_second = lax.broadcasted_iota(jnp.int32, (8, width), 0) == 6
    before = p_ref[:8] + jnp.where(at_second, mend, 0.0)
    w = [w_ref[i : i + 1] for i in range(w_ref.shape[0])]
    for at in strips(z_ref.shape[0]):
        p = p_ref[8 + at.start : 8 + at.stop]
        z_ref[at] = filtered(p, before, w)
        before = p[-8:]


def sums_kernel(
    scale, g_ref, u_ref, halo_ref, h_ref, us_ref, z_ref, gate_ref, w_ref, short_ref, inverse_ref,
    d_ref, dq_ref, sums_ref, *scratch
):
    high_d, low_d, high_c, low_c = scratch
    extent = h_ref.shape[0]
    rows, width = u_ref.shape
    taps = gate_ref.shape[0]
    blocks = rows // extent
    gate = [gate_ref[i : i + 1] for i in range(taps)]
    w = [w_ref[i : i + 1] for i in range(taps)]
    gate_sums = [jnp.zeros((8, width), F32) for _ in range(taps)]
    ahead = halo_ref[halo_ref.shape[0] - STRIP :].astype(F32)
    before = ahead[8:]
    first = halo_ref[halo_ref.shape[0] - extent - STRIP : halo_ref.shape[0] - extent].astype(F32)
    preceding = [first[STRIP - 1 :], ahead[STRIP - 1 :]]
    mend = None
    for at in strips(rows):
        g, u = g_ref[at].astype(F32), u_ref[at].astype(F32)
        late = [u] + [delayed(before, u, i) for i in range(1, taps)]
        before = u[8:]
        q = gate[0] * u
        for i in range(1, taps):
            q = q + gate[i] * late[i]
        dz, dq = g * q, g * z_ref[at]
        dq_ref[at] = dq
        put_halves(dz, high_d, low_d, at)
        gate_sums = [total + folded(dq * x) for total, x in zip(gate_sums, late)]
        if at.start % extent == 0:
            b, start = at.start // extent, dz[:1]
            if b >= 2:
                preceding.append(u_ref[(b - 1) * extent - STRIP : (b - 1) * extent].astype(F32)[STRIP - 1 :])
        if at.stop % extent == 0:
            term = start * (u[STRIP - 1 :] + preceding[b])
            mend = term if mend is None else mend + term
    for b in range(blocks):
        window = slice(b * extent, (b + 1) * extent)
        d_ref[b] = product(short_ref[...], stacked_rows(high_d, low_d, window))
    for at in strips(extent):
        im = slice(extent + at.start, extent + at.stop)
        cr = ci = None
        for b in range(blocks):
            dr, di, ur, ui = d_ref[b, at], d_ref[b, im], us_ref[b, at], us_ref[b, im]
            real, imaginary = dr * ur + di * ui, di * ur - dr * ui
            cr, ci = (real, imaginary) if cr is None else (cr + real, ci + imaginary)
        put_halves(cr, high_c, low_c, at)
        put_halves(ci, high_c, low_c, im)
    lags = product(inverse_ref[: extent + 8], stacked_rows(high_c, low_c)) * scale
    at_last = lax.broadcasted_iota(jnp.int32, (8, width), 0) == 1
    after = lags[extent:] + jnp.where(at_last, mend * scale, 0.0)
    value_sums = [jnp.zeros((8, width), F32) for _ in range(taps)]
    for row in range(extent - STRIP, -1, -STRIP):
        c = lags[row : row + STRIP]
        early = [c] + [advanced(c, after, i) for i in range(1, taps)]
        after = c[:8]
        total = w[0] * c
        for i in range(1, taps):
            total = total + w[i] * early[i]
        sums_ref[row : row + STRIP] = total
        h = h_ref[row : row + STRIP]
        value_sums = [sums + folded(h * x) for sums, x in zip(value_sums, early)]
    rest = [jnp.sum(x, axis=0, keepdims=True) * scale for x in gate_sums]
    rest += [jnp.sum(x, axis=0, keepdims=True) for x in value_sums]
    spare = sums_ref.shape[0] - extent - 2 * taps
    rest.append(jnp.zeros((spare, width), F32))
    sums_ref[extent:] = jnp.concatenate(rest, axis=0)


def input_kernel(
    lead, d_ref, dq_ref, hs_ref, gate_ref, w_ref, inverse_ref, grad_ref, end_ref, head_ref, *scratch
):
    high_r, low_r, r_ref = scratch
    extent = hs_ref.shape[0] // 2
    rows, width = dq_ref.shape
    taps = gate_ref.shape[0]
    blocks = rows // extent
    for at in strips(extent):
        im = slice(extent + at.start, extent + at.stop)
        hr, hi = hs_ref[at], hs_ref[im]
        for b in range(blocks):
            dr, di = d_ref[b, at], d_ref[b, im]
            put_halves(dr * hr + di * hi, high_r.at[b], low_r.at[b], at)
            put_halves(di * hr - dr * hi, high_r.at[b], low_r.at[b], im)
    for b in range(blocks):
        r_ref[b] = product(inverse_ref[...], stacked_rows(high_r.at[b], low_r.at[b]))
    w = [-w_ref[i : i + 1] for i in range(taps)]
    gate = [gate_ref[i : i + 1] for i in range(taps)]
    nothing = jnp.zeros((STRIP, width), F32)
    after_r = after_dq = nothing[:8]
    for row in range(rows - STRIP, -lead - 1, -STRIP):
        block, at = (row + extent) // extent, (row + extent) % extent
        if row < -extent:
            r = nothing
        elif block == 0:
            r = r_ref[0, at : at + STRIP]
        elif block == blocks:
            r = r_ref[blocks - 1, extent + at : extent + at + STRIP]
        else:
            r = r_ref[block - 1, extent + at : extent + at + STRIP] + r_ref[block, at : at + STRIP]
        total = w[0] * r
        for i in range(1, taps):
            total = total + w[i] * advanced(r, after_r, i)
        after_r = r[:8]
        if row >= -STRIP:
            dq = dq_ref[row : row + STRIP] if row >= 0 else nothing
            if row >= 0:
                total = total + gate[0] * dq
            for i in range(1, taps):
                total = total + gate[i] * advanced(dq, after_dq, i)
            after_dq = dq[:8]
        if row < 0:
            head_ref[lead + row : lead + row + STRIP] = total.astype(BF16)
        elif row < rows - lead:
            grad_ref[row : row + STRIP] = total.astype(BF16)
        else:
            end_ref[row - rows + lead : row - rows + lead + STRIP] = total


IN_VMEM = pl.BlockSpec(memory_space=pltpu.VMEM)
IN_SMEM = pl.BlockSpec(memory_space=pltpu.SMEM)
ANYWHERE = pl.BlockSpec(memory_space=pl.ANY)


def place_of(me_ref, k, pieces, piece):
    return pl.ds(pl.multiple_of(lax.rem(me_ref[0] + (pieces - k), pieces) * piece, piece), piece)


def call(name, body, inputs, constants, outs, scratch, block, cost, me, pieces=()):
    moved = [isinstance(x, list) for x in inputs]
    arrays = [x[0] if isinstance(x, list) else x for x in inputs]
    put = [isinstance(x, list) for x in outs]
    shapes = [x[0] if isinstance(x, list) else x for x in outs]
    width = shapes[0].shape[-1]
    blocks = width // block
    n_pieces, n_in, n_const, n_out = len(pieces), len(arrays), len(constants), len(shapes)
    held = [x for x, move in zip(arrays, moved) if move] + list(constants)
    held += [x for x, move in zip(shapes, put) if move]
    if pieces:
        held.append(jax.ShapeDtypeStruct((n_pieces * pieces[0].shape[0], width), pieces[0].dtype))

    def kernel(*refs):
        me_ref, piece_refs, refs = refs[0], refs[1 : 1 + n_pieces], refs[1 + n_pieces :]
        given, refs = refs[: n_in + n_const], refs[n_in + n_const :]
        results, refs = refs[:n_out], refs[n_out:]
        temporary, kept, sems, const_sems = refs[: len(scratch)], list(refs[len(scratch) : -2]), *refs[-2:]
        ins, sources, sinks = [], [], []
        for ref, move in zip(given, moved):
            ins.append(kept.pop(0) if move else ref)
            if move:
                sources.append((ref, ins[-1]))
        whole = [kept.pop(0) for _ in range(n_const)]
        shown = []
        for ref, move in zip(results, put):
            shown.append(kept.pop(0) if move else ref)
            if move:
                sinks.append((shown[-1], ref))
        if pieces:
            ins.insert(0, kept.pop(0))
            sources += [
                (ref, ins[0].at[place_of(me_ref, k, n_pieces, ref.shape[0])]) for k, ref in enumerate(piece_refs)
            ]

        def cut(ref, j):
            place = pl.ds(pl.multiple_of(j * block, block), block)
            return ref.at[(slice(None),) * (len(ref.shape) - 1) + (place,)]

        def copies(pairs, j, first):
            return [
                pltpu.make_async_copy(cut(a, j), cut(b, j), sems.at[first + i, j]) for i, (a, b) in enumerate(pairs)
            ]

        constant_copies = [
            pltpu.make_async_copy(a, b, const_sems.at[i]) for i, (a, b) in enumerate(zip(given[n_in:], whole))
        ]
        for copy in constant_copies:
            copy.start()
        for j in range(blocks):
            for copy in copies(sources, j, 0):
                copy.start()
        for copy in constant_copies:
            copy.wait()

        def one(j):
            for copy in copies(sources, j, 0):
                copy.wait()
            body(*[cut(x, j) for x in ins], *whole, *[cut(x, j) for x in shown], *temporary)
            for copy in copies(sinks, j, len(sources)):
                copy.start()

        pl.loop(0, blocks)(one)
        for j in range(blocks):
            for copy in copies(sinks, j, len(sources)):
                copy.wait()

    return pl.pallas_call(
        kernel,
        in_specs=[IN_SMEM]
        + [ANYWHERE] * n_pieces
        + [ANYWHERE if move else IN_VMEM for move in moved]
        + [ANYWHERE] * n_const,
        out_specs=[ANYWHERE if move else IN_VMEM for move in put],
        scratch_shapes=[pltpu.VMEM(shape, dtype) for shape, dtype in scratch]
        + [pltpu.VMEM(x.shape, x.dtype) for x in held]
        + [
            pltpu.SemaphoreType.DMA((n_pieces + sum(moved) + sum(put) + 1, blocks)),
            pltpu.SemaphoreType.DMA((n_const,)),
        ],
        out_shape=shapes,
        compiler_params=pltpu.CompilerParams(vmem_limit_bytes=VMEM_LIMIT),
        cost_estimate=cost,
        name=name,
    )(me, *pieces, *arrays, *constants)


def tail_step(pieces, me, lead):
    piece, width = pieces[0].shape
    rows = piece * len(pieces)

    def kernel(me_ref, *refs):
        tail_ref, held, sems, sem = refs[len(pieces) :]
        copies = [
            pltpu.make_async_copy(ref, held.at[place_of(me_ref, k, len(pieces), piece)], sems.at[k])
            for k, ref in enumerate(refs[: len(pieces)])
        ]
        for copy in copies:
            copy.start()
        for copy in copies:
            copy.wait()
        out = pltpu.make_async_copy(held.at[pl.ds(rows - lead, lead), :], tail_ref, sem)
        out.start()
        out.wait()

    return pl.pallas_call(
        kernel,
        in_specs=[IN_SMEM] + [ANYWHERE] * len(pieces),
        out_specs=ANYWHERE,
        scratch_shapes=[
            pltpu.VMEM((rows, width), BF16),
            pltpu.SemaphoreType.DMA((len(pieces),)),
            pltpu.SemaphoreType.DMA,
        ],
        out_shape=jax.ShapeDtypeStruct((lead, width), BF16),
        compiler_params=pltpu.CompilerParams(vmem_limit_bytes=VMEM_LIMIT),
        cost_estimate=BRIEF,
        name="tail_step",
    )(me, *pieces)


def signal_step(u_pieces, me, halo, h, w, matrices, block):
    width = h.shape[1]
    rows, extent = u_pieces[0].shape[0] * len(u_pieces), h.shape[0]
    blocks = rows // extent
    outs = [
        jax.ShapeDtypeStruct((blocks, 2 * extent, width), F32),
        jax.ShapeDtypeStruct((2 * extent, width), F32),
        jax.ShapeDtypeStruct((rows, width), F32),
        jax.ShapeDtypeStruct((rows, width), BF16),
    ]
    scratch = [((extent, block), BF16)] * 2 + [((blocks, 2 * extent, block), BF16)] * 2
    scratch += [((8 + rows, block), F32)]
    constants = [matrices[name] for name in ("both", "short", "around")]

    def body(u_ref, *refs):
        refs[9][...] = u_ref[...]
        signal_kernel(u_ref, *refs[:9], *refs[10:])

    return call(
        "signal_step", body, [[halo], [h], [w]], constants, outs, scratch, block, BRIEF, me, u_pieces
    )


def gradient_step(g_pieces, me, u, halo, h, us, hs, z, gate, w, matrices, scale, block):
    rows, width = u.shape
    extent, taps, lead = h.shape[0], gate.shape[0], halo.shape[0]
    blocks = rows // extent
    outs = [
        jax.ShapeDtypeStruct((extent + -(-2 * taps // 8) * 8, width), F32),
        jax.ShapeDtypeStruct((rows - lead, width), BF16),
        jax.ShapeDtypeStruct((lead, width), F32),
        jax.ShapeDtypeStruct((lead, width), BF16),
    ]
    spectra = (blocks, 2 * extent, block)
    scratch = [(spectra, F32), ((rows, block), F32)]
    scratch += [((rows, block), BF16)] * 2 + [((2 * extent, block), BF16)] * 2
    scratch += [(spectra, BF16)] * 2 + [(spectra, F32)]

    def body(g, u, halo, h, us, hs, z, gate, w, short, inverse, sums, grad, end, head, d, dq, *temporary):
        sums_kernel(scale, g, u, halo, h, us, z, gate, w, short, inverse, d, dq, sums, *temporary[:4])
        input_kernel(lead, d, dq, hs, gate, w, inverse, grad, end, head, *temporary[4:])

    return call(
        "gradient_step", body, [u, [halo], [h], us, hs, z, [gate], [w]],
        [matrices[name] for name in ("short", "inverse")], outs, scratch, block, LONG, me, g_pieces,
    )


def slices(x, axis, start, part):
    count = lax.axis_size(axis)
    me = lax.axis_index(axis)
    width = x.shape[1] // count
    return [
        lax.dynamic_slice_in_dim(x, lax.rem(me + k, count) * width + start, part, axis=1)
        for k in range(count)
    ]


def exchange(pieces, axis):
    count = lax.axis_size(axis)
    got = [pieces[0]] + [None] * (count - 1)
    for k in sorted(range(1, count), key=lambda k: abs(2 * k - count)):
        got[k] = lax.ppermute(pieces[k], axis, [(i, (i + k) % count) for i in range(count)])
    return got


def shifted(x, axis, by):
    count = lax.axis_size(axis)
    pairs = [(i, i + by) for i in range(count) if 0 <= i + by < count]
    return lax.ppermute(x, axis, pairs)


def at_once(exchange_of, x, axis):
    return lax.cond(lax.axis_index(axis) >= 0, exchange_of, lambda x: x, x)


def partner(x, axis, bit):
    count = lax.axis_size(axis)
    return lax.ppermute(x, axis, [(i, i ^ bit) for i in range(count)])


def summed(x, axis):
    total, bit, count = x + partner(x, axis, 1), 2, lax.axis_size(axis)
    while bit < count:
        short = total.astype(BF16)
        total = short.astype(F32) + partner(short, axis, bit).astype(F32)
        bit *= 2
    return total


def finish_step(terms, mine, sizes):
    part = terms[0].shape[1]
    width = part * len(terms)

    def kernel(mine_ref, *refs):
        terms, outs, held, sems = refs[:4], refs[4 : 4 + len(sizes)], refs[4 + len(sizes) : -1], refs[-1]
        copies = []
        for k, term in enumerate(terms):
            place = pl.ds(pl.multiple_of((mine_ref[0] ^ k) * part, part), part)
            x, row = term[...].astype(F32), 0
            for i, (size, out, ref) in enumerate(zip(sizes, outs, held)):
                ref[:, place] = x[row : row + size]
                row += size
                copies.append(pltpu.make_async_copy(ref.at[:, place], out.at[:, place], sems.at[i, k]))
                copies[-1].start()
        for copy in copies:
            copy.wait()

    return pl.pallas_call(
        kernel,
        in_specs=[IN_SMEM] + [IN_VMEM] * 4,
        out_specs=[ANYWHERE] * len(sizes),
        scratch_shapes=[pltpu.VMEM((size, width), F32) for size in sizes]
        + [pltpu.SemaphoreType.DMA((len(sizes), 4))],
        out_shape=[jax.ShapeDtypeStruct((size, width), F32) for size in sizes],
        compiler_params=pltpu.CompilerParams(vmem_limit_bytes=VMEM_LIMIT),
        cost_estimate=BRIEF,
        name="finish_step",
    )(mine, *terms)


def shards(out_grad, saved_input, explicit_filter_weights, gate_taps, value_featurizer_weights):
    extent, width = explicit_filter_weights.shape
    taps = gate_taps.shape[0]
    me = lax.axis_index("tp").astype(jnp.int32).reshape(1)
    rows = out_grad.shape[0] * lax.axis_size("tp")
    lead = -(-(extent + taps - 2) // 16) * 16
    block = min(BLOCK, width)
    matrices = {name: jnp.asarray(m) for name, m in transforms(extent).items()}
    scale = 1.0 / math.sqrt(rows * lax.axis_size("ctx"))
    h, gate, w = explicit_filter_weights, gate_taps, value_featurizer_weights
    u_pieces = exchange(slices(saved_input, "tp", 0, width), "tp")
    g_slices = slices(out_grad, "tp", 0, width)
    u_pieces, g_slices = lax.optimization_barrier((u_pieces, g_slices))
    g_pieces = exchange(g_slices, "tp")
    tail = tail_step(u_pieces, me, lead)
    halo = at_once(lambda x: shifted(x, "ctx", 1), tail, "ctx")
    us, hs, z, u = signal_step(u_pieces, me, halo, h, w, matrices, block)
    partial, main, end, head = gradient_step(
        g_pieces, me, u, halo, h, us, hs, z, gate, w, matrices, scale, block
    )
    incoming = shifted(head, "ctx", -1)
    sizes = (extent, taps, taps)
    if lax.axis_size("ctx") == 8:
        mine = (lax.axis_index("ctx") // 2).astype(jnp.int32)
        part = width // 4
        quarters = [lax.dynamic_slice_in_dim(partial, (mine ^ k) * part, part, axis=1) for k in range(4)]
        got = [partner(quarters[k].astype(BF16), "ctx", 2 * k) for k in range(1, 4)]
        total = (quarters[0] + got[0].astype(F32)) + (got[1].astype(F32) + got[2].astype(F32))
        total = total + partner(total, "ctx", 1)
        total, incoming = lax.optimization_barrier((total, incoming))
        total = total.astype(BF16)
        terms = [total] + [partner(total, "ctx", 2 * k) for k in range(1, 4)]
        sums = finish_step(terms, mine.reshape(1), sizes)
    else:
        total = summed(partial, "ctx")
        ends = np.cumsum(sizes)
        sums = [total[stop - size : stop] for size, stop in zip(sizes, ends)]
    end = (end + incoming.astype(F32)).astype(BF16)
    return (jnp.concatenate([main, end], axis=0), *sums)


def solution(mesh):
    placed = (
        P(("ctx", "tp"), None),
        P(("ctx", "tp"), None),
        P(None, "tp"),
        P(None, "tp"),
        P(None, "tp"),
    )
    return jax.shard_map(
        shards,
        mesh=mesh,
        in_specs=placed,
        out_specs=(P("ctx", "tp"), P(None, "tp"), P(None, "tp"), P(None, "tp")),
        check_vma=False,
    )
```

```python
import math

import jax
import jax.numpy as jnp
import numpy as np
from jax import lax
from jax.experimental import pallas as pl
from jax.experimental.pallas import tpu as pltpu
from jax.sharding import PartitionSpec as P

F32 = jnp.float32
BF16 = jnp.bfloat16
VMEM_LIMIT = 16 * 1024 * 1024
BLOCK = 1024
BRIEF = pl.CostEstimate(flops=1000, bytes_accessed=1000, transcendentals=0)
LONG = pl.CostEstimate(flops=20_000_000_000, bytes_accessed=100_000_000, transcendentals=0)


STRIP = 16


def strips(rows):
    return [slice(i, i + STRIP) for i in range(0, rows, STRIP)]


def put_halves(x, high_ref, low_ref, rows):
    high = x.astype(BF16)
    high_ref[rows] = high
    low_ref[rows] = (x - high.astype(F32)).astype(BF16)


def stacked_rows(high_ref, low_ref, rows=slice(None)):
    high = high_ref[rows]
    return jnp.concatenate([high, high, low_ref[rows]], axis=0)


def product(matrix, x):
    return jnp.dot(matrix, x, preferred_element_type=F32)


def transforms(extent):
    points = 2 * extent
    angle = np.pi * np.outer(2 * np.arange(extent) + 1, np.arange(points)) / points
    whole = np.concatenate([np.cos(angle), -np.sin(angle)])
    back = whole.T / extent

    def split(matrix, terms=3):
        high = matrix.astype(jnp.bfloat16)
        low = (matrix - high.astype(np.float64)).astype(jnp.bfloat16)
        return np.concatenate([high, low, high][:terms], axis=1)

    return {
        "both": split(whole, 2),
        "short": split(whole[:, :extent]),
        "inverse": split(np.concatenate([-back[extent:], back[:extent]])),
        "around": split(-back[extent - 8 :]),
    }


def delayed(before, x, by):
    return pltpu.roll(jnp.concatenate([before, x], axis=0), by, 0)[8:]


def advanced(x, after, by):
    both = jnp.concatenate([x, after], axis=0)
    return pltpu.roll(both, both.shape[0] - by, 0)[: x.shape[0]]


def folded(x):
    return sum(x[i : i + 8] for i in range(8, x.shape[0], 8)) + x[:8]


def filtered(u, before, taps):
    value = taps[0] * u
    for j in range(1, len(taps)):
        value = value + taps[j] * delayed(before, u, j)
    return value


def convolved(matrix, spectrum, hs_ref, high_ref, low_ref):
    for at in strips(hs_ref.shape[0] // 2):
        im = slice(at.start + hs_ref.shape[0] // 2, at.stop + hs_ref.shape[0] // 2)
        ur, ui, hr, hi = spectrum[at], spectrum[im], hs_ref[at], hs_ref[im]
        put_halves(ur * hr - ui * hi, high_ref, low_ref, at)
        put_halves(ur * hi + ui * hr, high_ref, low_ref, im)
    return product(matrix, stacked_rows(high_ref, low_ref))


def twice(x):
    return jnp.concatenate([x, x], axis=0)


def signal_kernel(
    u_ref, halo_ref, h_ref, w_ref, both_ref, short_ref, around_ref, us_ref, hs_ref, z_ref, *scratch
):
    high_h, low_h, high_p, low_p, p_ref = scratch
    extent = h_ref.shape[0]
    lead, width = halo_ref.shape
    blocks = us_ref.shape[0]
    for at in strips(extent):
        put_halves(-h_ref[at], high_h, low_h, at)
    hs_ref[...] = product(short_ref[...], stacked_rows(high_h, low_h))
    for b in range(blocks):
        last = u_ref[b * extent : (b + 1) * extent]
        first = halo_ref[lead - extent :] if b == 0 else u_ref[(b - 1) * extent : b * extent]
        us_ref[b] = product(both_ref[...], jnp.concatenate([first, last] * 2, axis=0))
    for b in range(blocks):
        matrix = around_ref[...] if b == 0 else around_ref[8:]
        rows = slice(0, extent + 8) if b == 0 else slice(8 + b * extent, 8 + (b + 1) * extent)
        p_ref[rows] = convolved(matrix, us_ref.at[b], hs_ref, high_p.at[b], low_p.at[b])
    ahead = halo_ref[lead - extent - STRIP : lead - extent].astype(F32)[STRIP - 1 :]
    final = u_ref[extent - STRIP : extent].astype(F32)[STRIP - 1 :]
    mend = h_ref[extent - 1 : extent] * (ahead + final)
    at_second = lax.broadcasted_iota(jnp.int32, (8, width), 0) == 6
    before = p_ref[:8] + jnp.where(at_second, mend, 0.0)
    w = [w_ref[i : i + 1] for i in range(w_ref.shape[0])]
    for at in strips(z_ref.shape[0]):
        p = p_ref[8 + at.start : 8 + at.stop]
        z_ref[at] = filtered(p, before, w)
        before = p[-8:]


def sums_kernel(
    scale, g_ref, u_ref, halo_ref, h_ref, us_ref, z_ref, gate_ref, w_ref, short_ref, inverse_ref,
    d_ref, dq_ref, sums_ref, *scratch
):
    high_d, low_d, high_c, low_c = scratch
    extent = h_ref.shape[0]
    rows, width = u_ref.shape
    taps = gate_ref.shape[0]
    blocks = rows // extent
    gate = [gate_ref[i : i + 1] for i in range(taps)]
    w = [w_ref[i : i + 1] for i in range(taps)]
    gate_sums = [jnp.zeros((8, width), F32) for _ in range(taps)]
    ahead = halo_ref[halo_ref.shape[0] - STRIP :].astype(F32)
    before = ahead[8:]
    first = halo_ref[halo_ref.shape[0] - extent - STRIP : halo_ref.shape[0] - extent].astype(F32)
    preceding = [first[STRIP - 1 :], ahead[STRIP - 1 :]]
    mend = None
    for at in strips(rows):
        g, u = g_ref[at].astype(F32), u_ref[at].astype(F32)
        late = [u] + [delayed(before, u, i) for i in range(1, taps)]
        before = u[8:]
        q = gate[0] * u
        for i in range(1, taps):
            q = q + gate[i] * late[i]
        dz, dq = g * q, g * z_ref[at]
        dq_ref[at] = dq
        put_halves(dz, high_d, low_d, at)
        gate_sums = [total + folded(dq * x) for total, x in zip(gate_sums, late)]
        if at.start % extent == 0:
            b, start = at.start // extent, dz[:1]
            if b >= 2:
                preceding.append(u_ref[(b - 1) * extent - STRIP : (b - 1) * extent].astype(F32)[STRIP - 1 :])
        if at.stop % extent == 0:
            term = start * (u[STRIP - 1 :] + preceding[b])
            mend = term if mend is None else mend + term
    for b in range(blocks):
        window = slice(b * extent, (b + 1) * extent)
        d_ref[b] = product(short_ref[...], stacked_rows(high_d, low_d, window))
    for at in strips(extent):
        im = slice(extent + at.start, extent + at.stop)
        cr = ci = None
        for b in range(blocks):
            dr, di, ur, ui = d_ref[b, at], d_ref[b, im], us_ref[b, at], us_ref[b, im]
            real, imaginary = dr * ur + di * ui, di * ur - dr * ui
            cr, ci = (real, imaginary) if cr is None else (cr + real, ci + imaginary)
        put_halves(cr, high_c, low_c, at)
        put_halves(ci, high_c, low_c, im)
    lags = product(inverse_ref[: extent + 8], stacked_rows(high_c, low_c)) * scale
    at_last = lax.broadcasted_iota(jnp.int32, (8, width), 0) == 1
    after = lags[extent:] + jnp.where(at_last, mend * scale, 0.0)
    value_sums = [jnp.zeros((8, width), F32) for _ in range(taps)]
    for row in range(extent - STRIP, -1, -STRIP):
        c = lags[row : row + STRIP]
        early = [c] + [advanced(c, after, i) for i in range(1, taps)]
        after = c[:8]
        total = w[0] * c
        for i in range(1, taps):
            total = total + w[i] * early[i]
        sums_ref[row : row + STRIP] = total
        h = h_ref[row : row + STRIP]
        value_sums = [sums + folded(h * x) for sums, x in zip(value_sums, early)]
    rest = [jnp.sum(x, axis=0, keepdims=True) * scale for x in gate_sums]
    rest += [jnp.sum(x, axis=0, keepdims=True) for x in value_sums]
    spare = sums_ref.shape[0] - extent - 2 * taps
    rest.append(jnp.zeros((spare, width), F32))
    sums_ref[extent:] = jnp.concatenate(rest, axis=0)


def input_kernel(
    lead, d_ref, dq_ref, hs_ref, gate_ref, w_ref, inverse_ref, grad_ref, end_ref, head_ref, *scratch
):
    high_r, low_r, r_ref = scratch
    extent = hs_ref.shape[0] // 2
    rows, width = dq_ref.shape
    taps = gate_ref.shape[0]
    blocks = rows // extent
    for at in strips(extent):
        im = slice(extent + at.start, extent + at.stop)
        hr, hi = hs_ref[at], hs_ref[im]
        for b in range(blocks):
            dr, di = d_ref[b, at], d_ref[b, im]
            put_halves(dr * hr + di * hi, high_r.at[b], low_r.at[b], at)
            put_halves(di * hr - dr * hi, high_r.at[b], low_r.at[b], im)
    for b in range(blocks):
        r_ref[b] = product(inverse_ref[...], stacked_rows(high_r.at[b], low_r.at[b]))
    w = [-w_ref[i : i + 1] for i in range(taps)]
    gate = [gate_ref[i : i + 1] for i in range(taps)]
    nothing = jnp.zeros((STRIP, width), F32)
    after_r = after_dq = nothing[:8]
    for row in range(rows - STRIP, -lead - 1, -STRIP):
        block, at = (row + extent) // extent, (row + extent) % extent
        if row < -extent:
            r = nothing
        elif block == 0:
            r = r_ref[0, at : at + STRIP]
        elif block == blocks:
            r = r_ref[blocks - 1, extent + at : extent + at + STRIP]
        else:
            r = r_ref[block - 1, extent + at : extent + at + STRIP] + r_ref[block, at : at + STRIP]
        total = w[0] * r
        for i in range(1, taps):
            total = total + w[i] * advanced(r, after_r, i)
        after_r = r[:8]
        if row >= -STRIP:
            dq = dq_ref[row : row + STRIP] if row >= 0 else nothing
            if row >= 0:
                total = total + gate[0] * dq
            for i in range(1, taps):
                total = total + gate[i] * advanced(dq, after_dq, i)
            after_dq = dq[:8]
        if row < 0:
            head_ref[lead + row : lead + row + STRIP] = total.astype(BF16)
        elif row < rows - lead:
            grad_ref[row : row + STRIP] = total.astype(BF16)
        else:
            end_ref[row - rows + lead : row - rows + lead + STRIP] = total


IN_VMEM = pl.BlockSpec(memory_space=pltpu.VMEM)
IN_SMEM = pl.BlockSpec(memory_space=pltpu.SMEM)
ANYWHERE = pl.BlockSpec(memory_space=pl.ANY)


def place_of(me_ref, k, pieces, piece):
    return pl.ds(pl.multiple_of(lax.rem(me_ref[0] + (pieces - k), pieces) * piece, piece), piece)


def call(name, body, inputs, constants, outs, scratch, block, cost, me, pieces=(), kept_outs=(), at_end=None):
    moved = [isinstance(x, list) for x in inputs]
    arrays = [x[0] if isinstance(x, list) else x for x in inputs]
    width = arrays[0].shape[-1]
    blocks = width // block
    last_outs = () if at_end is None else at_end[0]
    n_pieces, n_in, n_const = len(pieces), len(arrays), len(constants)
    n_out = len(outs) + len(last_outs)
    held = [x for x, move in zip(arrays, moved) if move] + list(constants) + list(kept_outs)
    if pieces:
        held.append(jax.ShapeDtypeStruct((n_pieces * pieces[0].shape[0], width), pieces[0].dtype))

    def kernel(*refs):
        me_ref, piece_refs, refs = refs[0], refs[1 : 1 + n_pieces], refs[1 + n_pieces :]
        given, refs = refs[: n_in + n_const], refs[n_in + n_const :]
        results, refs = refs[:n_out], refs[n_out:]
        temporary, kept, sems, const_sems = refs[: len(scratch)], list(refs[len(scratch) : -2]), *refs[-2:]
        ins, sources = [], []
        for ref, move in zip(given, moved):
            ins.append(kept.pop(0) if move else ref)
            if move:
                sources.append((ref, ins[-1]))
        whole = [kept.pop(0) for _ in range(n_const)]
        stay = [kept.pop(0) for _ in kept_outs]
        if pieces:
            ins.insert(0, kept.pop(0))
            sources += [
                (ref, ins[0].at[place_of(me_ref, k, n_pieces, ref.shape[0])]) for k, ref in enumerate(piece_refs)
            ]

        def cut(ref, j):
            place = pl.ds(pl.multiple_of(j * block, block), block)
            return ref.at[(slice(None),) * (len(ref.shape) - 1) + (place,)]

        def copies(j):
            return [pltpu.make_async_copy(cut(a, j), cut(b, j), sems.at[i, j]) for i, (a, b) in enumerate(sources)]

        constant_copies = [
            pltpu.make_async_copy(a, b, const_sems.at[i]) for i, (a, b) in enumerate(zip(given[n_in:], whole))
        ]
        for copy in constant_copies:
            copy.start()
        for j in range(blocks):
            for copy in copies(j):
                copy.start()
        for copy in constant_copies:
            copy.wait()

        def one(j):
            for copy in copies(j):
                copy.wait()
            shown = list(results[: len(outs)]) + stay
            body(*[cut(x, j) for x in ins], *whole, *[cut(x, j) for x in shown], *temporary)

        pl.loop(0, blocks)(one)
        if at_end is not None:
            at_end[1](me_ref, stay, results[len(outs) :])

    return pl.pallas_call(
        kernel,
        in_specs=[IN_SMEM]
        + [ANYWHERE] * n_pieces
        + [ANYWHERE if move else IN_VMEM for move in moved]
        + [ANYWHERE] * n_const,
        out_specs=[IN_VMEM] * n_out,
        scratch_shapes=[pltpu.VMEM(shape, dtype) for shape, dtype in scratch]
        + [pltpu.VMEM(x.shape, x.dtype) for x in held]
        + [
            pltpu.SemaphoreType.DMA((n_pieces + sum(moved) + 1, blocks)),
            pltpu.SemaphoreType.DMA((n_const,)),
        ],
        out_shape=[*outs, *last_outs],
        compiler_params=pltpu.CompilerParams(vmem_limit_bytes=VMEM_LIMIT),
        cost_estimate=cost,
        name=name,
    )(me, *pieces, *arrays, *constants)


def tail_step(pieces, me, lead):
    piece, width = pieces[0].shape
    rows = piece * len(pieces)

    def kernel(me_ref, *refs):
        tail_ref, held, sems, sem = refs[len(pieces) :]
        copies = [
            pltpu.make_async_copy(ref, held.at[place_of(me_ref, k, len(pieces), piece)], sems.at[k])
            for k, ref in enumerate(refs[: len(pieces)])
        ]
        for copy in copies:
            copy.start()
        for copy in copies:
            copy.wait()
        out = pltpu.make_async_copy(held.at[pl.ds(rows - lead, lead), :], tail_ref, sem)
        out.start()
        out.wait()

    return pl.pallas_call(
        kernel,
        in_specs=[IN_SMEM] + [ANYWHERE] * len(pieces),
        out_specs=ANYWHERE,
        scratch_shapes=[
            pltpu.VMEM((rows, width), BF16),
            pltpu.SemaphoreType.DMA((len(pieces),)),
            pltpu.SemaphoreType.DMA,
        ],
        out_shape=jax.ShapeDtypeStruct((lead, width), BF16),
        compiler_params=pltpu.CompilerParams(vmem_limit_bytes=VMEM_LIMIT),
        cost_estimate=BRIEF,
        name="tail_step",
    )(me, *pieces)


def signal_step(u_pieces, me, halo, h, w, matrices, block):
    width = h.shape[1]
    rows, extent = u_pieces[0].shape[0] * len(u_pieces), h.shape[0]
    blocks = rows // extent
    outs = [
        jax.ShapeDtypeStruct((blocks, 2 * extent, width), F32),
        jax.ShapeDtypeStruct((2 * extent, width), F32),
        jax.ShapeDtypeStruct((rows, width), F32),
        jax.ShapeDtypeStruct((rows, width), BF16),
    ]
    scratch = [((extent, block), BF16)] * 2 + [((blocks, 2 * extent, block), BF16)] * 2
    scratch += [((8 + rows, block), F32)]
    constants = [matrices[name] for name in ("both", "short", "around")]

    def body(u_ref, *refs):
        refs[9][...] = u_ref[...]
        signal_kernel(u_ref, *refs[:9], *refs[10:])

    return call(
        "signal_step", body, [[halo], [h], [w]], constants, outs, scratch, block, BRIEF, me, u_pieces
    )


def gradient_step(g_pieces, me, u, halo, h, us, hs, z, gate, w, matrices, scale, block, shares):
    rows, width = u.shape
    extent, taps, lead = h.shape[0], gate.shape[0], halo.shape[0]
    blocks = rows // extent
    count, part = extent + -(-2 * taps // 8) * 8, width // shares
    outs = [
        jax.ShapeDtypeStruct((rows - lead, width), BF16),
        jax.ShapeDtypeStruct((lead, width), F32),
        jax.ShapeDtypeStruct((lead, width), BF16),
    ]
    sums = [jax.ShapeDtypeStruct((count, width), F32)]
    spectra = (blocks, 2 * extent, block)
    scratch = [(spectra, F32), ((rows, block), F32)]
    scratch += [((rows, block), BF16)] * 2 + [((2 * extent, block), BF16)] * 2
    scratch += [(spectra, BF16)] * 2 + [(spectra, F32)]
    ends = [jax.ShapeDtypeStruct((count, part), BF16 if k else F32) for k in range(shares)]

    def body(g, u, halo, h, us, hs, z, gate, w, short, inverse, grad, end, head, sums, d, dq, *temporary):
        sums_kernel(scale, g, u, halo, h, us, z, gate, w, short, inverse, d, dq, sums, *temporary[:4])
        input_kernel(lead, d, dq, hs, gate, w, inverse, grad, end, head, *temporary[4:])

    def share(me_ref, kept, refs):
        for k, ref in enumerate(refs):
            start = pl.multiple_of((me_ref[1] ^ k) * part, part) if shares > 1 else 0
            ref[...] = kept[0][:, pl.ds(start, part)].astype(ref.dtype)

    main, end, head, *terms = call(
        "gradient_step", body, [u, [halo], [h], us, hs, z, [gate], [w]],
        [matrices[name] for name in ("short", "inverse")], outs, scratch, block, LONG, me, g_pieces, sums,
        (ends, share),
    )
    return main, end, head, terms


def slices(x, axis, start, part):
    count = lax.axis_size(axis)
    me = lax.axis_index(axis)
    width = x.shape[1] // count
    return [
        lax.dynamic_slice_in_dim(x, lax.rem(me + k, count) * width + start, part, axis=1)
        for k in range(count)
    ]


def exchange(pieces, axis):
    count = lax.axis_size(axis)
    got = [pieces[0]] + [None] * (count - 1)
    for k in sorted(range(1, count), key=lambda k: abs(2 * k - count)):
        got[k] = lax.ppermute(pieces[k], axis, [(i, (i + k) % count) for i in range(count)])
    return got


def shifted(x, axis, by):
    count = lax.axis_size(axis)
    pairs = [(i, i + by) for i in range(count) if 0 <= i + by < count]
    return lax.ppermute(x, axis, pairs)


def at_once(exchange_of, x, axis):
    return lax.cond(lax.axis_index(axis) >= 0, exchange_of, jnp.zeros_like, x)


def partner(x, axis, bit):
    count = lax.axis_size(axis)
    return lax.ppermute(x, axis, [(i, i ^ bit) for i in range(count)])


def summed(x, axis):
    total, bit, count = x + partner(x, axis, 1), 2, lax.axis_size(axis)
    while bit < count:
        short = total.astype(BF16)
        total = short.astype(F32) + partner(short, axis, bit).astype(F32)
        bit *= 2
    return total


def finish_step(terms, me, sizes):
    part, shares = terms[0].shape[1], len(terms)
    width = part * shares

    def kernel(me_ref, *refs):
        terms, outs, held, sems = refs[:shares], refs[shares : shares + len(sizes)], refs[shares + len(sizes) : -1], refs[-1]
        copies = []
        for k, term in enumerate(terms):
            place = pl.ds(pl.multiple_of((me_ref[1] ^ k) * part, part), part)
            x, row = term[...].astype(F32), 0
            for i, (size, out, ref) in enumerate(zip(sizes, outs, held)):
                ref[:, place] = x[row : row + size]
                row += size
                copies.append(pltpu.make_async_copy(ref.at[:, place], out.at[:, place], sems.at[i, k]))
                copies[-1].start()
        for copy in copies:
            copy.wait()

    return pl.pallas_call(
        kernel,
        in_specs=[IN_SMEM] + [IN_VMEM] * shares,
        out_specs=[ANYWHERE] * len(sizes),
        scratch_shapes=[pltpu.VMEM((size, width), F32) for size in sizes]
        + [pltpu.SemaphoreType.DMA((len(sizes), shares))],
        out_shape=[jax.ShapeDtypeStruct((size, width), F32) for size in sizes],
        compiler_params=pltpu.CompilerParams(vmem_limit_bytes=VMEM_LIMIT),
        cost_estimate=BRIEF,
        name="finish_step",
    )(me, *terms)


def shards(out_grad, saved_input, explicit_filter_weights, gate_taps, value_featurizer_weights):
    extent, width = explicit_filter_weights.shape
    taps = gate_taps.shape[0]
    me = jnp.stack([lax.axis_index("tp"), lax.axis_index("ctx") // 2]).astype(jnp.int32)
    rows = out_grad.shape[0] * lax.axis_size("tp")
    lead = -(-(extent + taps - 2) // 16) * 16
    block = min(BLOCK, width)
    matrices = {name: jnp.asarray(m) for name, m in transforms(extent).items()}
    scale = 1.0 / math.sqrt(rows * lax.axis_size("ctx"))
    h, gate, w = explicit_filter_weights, gate_taps, value_featurizer_weights
    u_pieces = exchange(slices(saved_input, "tp", 0, width), "tp")
    g_slices = slices(out_grad, "tp", 0, width)
    u_pieces, g_slices = lax.optimization_barrier((u_pieces, g_slices))
    g_pieces = exchange(g_slices, "tp")
    tail = tail_step(u_pieces, me, lead)
    halo = at_once(lambda x: shifted(x, "ctx", 1), tail, "ctx")
    us, hs, z, u = signal_step(u_pieces, me, halo, h, w, matrices, block)
    chips = lax.axis_size("ctx") // 2
    shares = chips if chips == 4 and width % (128 * chips) == 0 else 1
    main, end, head, terms = gradient_step(
        g_pieces, me, u, halo, h, us, hs, z, gate, w, matrices, scale, block, shares
    )
    sizes = (extent, taps, taps)
    if shares > 1:
        terms = [terms[0]] + [partner(terms[k], "ctx", 2 * k).astype(F32) for k in range(1, shares)]
        incoming = shifted(head, "ctx", -1)
        while len(terms) > 1:
            terms = [a + b for a, b in zip(terms[::2], terms[1::2])]
        total = terms[0] + partner(terms[0], "ctx", 1)
        total, incoming = lax.optimization_barrier((total, incoming))
        total = total.astype(BF16)
        terms = [total] + [partner(total, "ctx", 2 * k) for k in range(1, shares)]
        sums = finish_step(terms, me, sizes)
    else:
        incoming = shifted(head, "ctx", -1)
        total = summed(terms[0], "ctx")
        ends = np.cumsum(sizes)
        sums = [total[stop - size : stop] for size, stop in zip(sizes, ends)]
    end = (end + incoming.astype(F32)).astype(BF16)
    return (jnp.concatenate([main, end], axis=0), *sums)


def solution(mesh):
    placed = (
        P(("ctx", "tp"), None),
        P(("ctx", "tp"), None),
        P(None, "tp"),
        P(None, "tp"),
        P(None, "tp"),
    )
    return jax.shard_map(
        shards,
        mesh=mesh,
        in_specs=placed,
        out_specs=(P("ctx", "tp"), P(None, "tp"), P(None, "tp"), P(None, "tp")),
        check_vma=False,
    )
```

```python
import math

import jax
import jax.numpy as jnp
import numpy as np
from jax import lax
from jax.experimental import pallas as pl
from jax.experimental.pallas import tpu as pltpu
from jax.sharding import PartitionSpec as P

F32 = jnp.float32
BF16 = jnp.bfloat16
VMEM_LIMIT = 16 * 1024 * 1024
BLOCK = 1024
BRIEF = pl.CostEstimate(flops=1000, bytes_accessed=1000, transcendentals=0)
LONG = pl.CostEstimate(flops=20_000_000_000, bytes_accessed=100_000_000, transcendentals=0)


STRIP = 16


def strips(rows):
    return [slice(i, i + STRIP) for i in range(0, rows, STRIP)]


def put_halves(x, high_ref, low_ref, rows):
    high = x.astype(BF16)
    high_ref[rows] = high
    low_ref[rows] = (x - high.astype(F32)).astype(BF16)


def stacked_rows(high_ref, low_ref, rows=slice(None)):
    high = high_ref[rows]
    return jnp.concatenate([high, high, low_ref[rows]], axis=0)


def product(matrix, x):
    return jnp.dot(matrix, x, preferred_element_type=F32)


def transforms(extent):
    points = 2 * extent
    angle = np.pi * np.outer(2 * np.arange(extent) + 1, np.arange(points)) / points
    whole = np.concatenate([np.cos(angle), -np.sin(angle)])
    back = whole.T / extent

    def split(matrix, terms=3):
        high = matrix.astype(jnp.bfloat16)
        low = (matrix - high.astype(np.float64)).astype(jnp.bfloat16)
        return np.concatenate([high, low, high][:terms], axis=1)

    return {
        "both": split(whole, 2),
        "short": split(whole[:, :extent]),
        "inverse": split(np.concatenate([-back[extent:], back[:extent]])),
        "around": split(-back[extent - STRIP :]),
    }


def delayed(before, x, by):
    return pltpu.roll(jnp.concatenate([before, x], axis=0), by, 0)[8:]


def advanced(x, after, by):
    both = jnp.concatenate([x, after], axis=0)
    return pltpu.roll(both, both.shape[0] - by, 0)[: x.shape[0]]


def folded(x):
    return sum(x[i : i + 8] for i in range(8, x.shape[0], 8)) + x[:8]


def filtered(u, before, taps):
    value = taps[0] * u
    for j in range(1, len(taps)):
        value = value + taps[j] * delayed(before, u, j)
    return value


def convolved(matrix, spectrum, hs_ref, high_ref, low_ref):
    for at in strips(hs_ref.shape[0] // 2):
        im = slice(at.start + hs_ref.shape[0] // 2, at.stop + hs_ref.shape[0] // 2)
        ur, ui, hr, hi = spectrum[at], spectrum[im], hs_ref[at], hs_ref[im]
        put_halves(ur * hr - ui * hi, high_ref, low_ref, at)
        put_halves(ur * hi + ui * hr, high_ref, low_ref, im)
    return product(matrix, stacked_rows(high_ref, low_ref))


def twice(x):
    return jnp.concatenate([x, x], axis=0)


def signal_kernel(
    u_ref, halo_ref, h_ref, w_ref, both_ref, short_ref, around_ref, us_ref, hs_ref, z_ref, *scratch
):
    high_h, low_h, high_p, low_p, p_ref = scratch
    extent = h_ref.shape[0]
    lead, width = halo_ref.shape
    blocks = us_ref.shape[0]
    for at in strips(extent):
        put_halves(-h_ref[at], high_h, low_h, at)
    hs_ref[...] = product(short_ref[...], stacked_rows(high_h, low_h))
    for b in range(blocks):
        last = u_ref[b * extent : (b + 1) * extent]
        first = halo_ref[lead - extent :] if b == 0 else u_ref[(b - 1) * extent : b * extent]
        us_ref[b] = product(both_ref[...], jnp.concatenate([first, last] * 2, axis=0))
    for b in range(blocks):
        matrix = around_ref[...] if b == 0 else around_ref[STRIP:]
        rows = slice(0 if b == 0 else STRIP + b * extent, STRIP + (b + 1) * extent)
        p_ref[rows] = convolved(matrix, us_ref.at[b], hs_ref, high_p.at[b], low_p.at[b])
    ahead = halo_ref[lead - extent - STRIP : lead - extent].astype(F32)[STRIP - 1 :]
    final = u_ref[extent - STRIP : extent].astype(F32)[STRIP - 1 :]
    mend = h_ref[extent - 1 : extent] * (ahead + final)
    at_second = lax.broadcasted_iota(jnp.int32, (8, width), 0) == 6
    before = p_ref[8:STRIP] + jnp.where(at_second, mend, 0.0)
    w = [w_ref[i : i + 1] for i in range(w_ref.shape[0])]
    for at in strips(z_ref.shape[0]):
        p = p_ref[STRIP + at.start : STRIP + at.stop]
        z_ref[at] = filtered(p, before, w)
        before = p[-8:]


def sums_kernel(
    scale, g_ref, u_ref, halo_ref, h_ref, us_ref, z_ref, gate_ref, w_ref, short_ref, inverse_ref,
    d_ref, dq_ref, sums_ref, *scratch
):
    high_d, low_d, high_c, low_c = scratch
    extent = h_ref.shape[0]
    rows, width = u_ref.shape
    taps = gate_ref.shape[0]
    blocks = rows // extent
    gate = [gate_ref[i : i + 1] for i in range(taps)]
    w = [w_ref[i : i + 1] for i in range(taps)]
    gate_sums = [jnp.zeros((8, width), F32) for _ in range(taps)]
    ahead = halo_ref[halo_ref.shape[0] - STRIP :].astype(F32)
    before = ahead[8:]
    first = halo_ref[halo_ref.shape[0] - extent - STRIP : halo_ref.shape[0] - extent].astype(F32)
    preceding = [first[STRIP - 1 :], ahead[STRIP - 1 :]]
    mend = None
    for at in strips(rows):
        g, u = g_ref[at].astype(F32), u_ref[at].astype(F32)
        late = [u] + [delayed(before, u, i) for i in range(1, taps)]
        before = u[8:]
        q = gate[0] * u
        for i in range(1, taps):
            q = q + gate[i] * late[i]
        dz, dq = g * q, g * z_ref[at]
        dq_ref[at] = dq
        put_halves(dz, high_d, low_d, at)
        gate_sums = [total + folded(dq * x) for total, x in zip(gate_sums, late)]
        if at.start % extent == 0:
            b, start = at.start // extent, dz[:1]
            if b >= 2:
                preceding.append(u_ref[(b - 1) * extent - STRIP : (b - 1) * extent].astype(F32)[STRIP - 1 :])
        if at.stop % extent == 0:
            term = start * (u[STRIP - 1 :] + preceding[b])
            mend = term if mend is None else mend + term
    for b in range(blocks):
        window = slice(b * extent, (b + 1) * extent)
        d_ref[b] = product(short_ref[...], stacked_rows(high_d, low_d, window))
    for at in strips(extent):
        im = slice(extent + at.start, extent + at.stop)
        cr = ci = None
        for b in range(blocks):
            dr, di, ur, ui = d_ref[b, at], d_ref[b, im], us_ref[b, at], us_ref[b, im]
            real, imaginary = dr * ur + di * ui, di * ur - dr * ui
            cr, ci = (real, imaginary) if cr is None else (cr + real, ci + imaginary)
        put_halves(cr, high_c, low_c, at)
        put_halves(ci, high_c, low_c, im)
    lags = product(inverse_ref[: extent + STRIP], stacked_rows(high_c, low_c)) * scale
    at_last = lax.broadcasted_iota(jnp.int32, (8, width), 0) == 1
    after = lags[extent : extent + 8] + jnp.where(at_last, mend * scale, 0.0)
    value_sums = [jnp.zeros((8, width), F32) for _ in range(taps)]
    for row in range(extent - STRIP, -1, -STRIP):
        c = lags[row : row + STRIP]
        early = [c] + [advanced(c, after, i) for i in range(1, taps)]
        after = c[:8]
        total = w[0] * c
        for i in range(1, taps):
            total = total + w[i] * early[i]
        sums_ref[row : row + STRIP] = total
        h = h_ref[row : row + STRIP]
        value_sums = [sums + folded(h * x) for sums, x in zip(value_sums, early)]
    rest = [jnp.sum(x, axis=0, keepdims=True) * scale for x in gate_sums]
    rest += [jnp.sum(x, axis=0, keepdims=True) for x in value_sums]
    spare = sums_ref.shape[0] - extent - 2 * taps
    rest.append(jnp.zeros((spare, width), F32))
    sums_ref[extent:] = jnp.concatenate(rest, axis=0)


def input_kernel(
    lead, d_ref, dq_ref, hs_ref, gate_ref, w_ref, inverse_ref, grad_ref, end_ref, head_ref, *scratch
):
    high_r, low_r, r_ref = scratch
    extent = hs_ref.shape[0] // 2
    rows, width = dq_ref.shape
    taps = gate_ref.shape[0]
    blocks = rows // extent
    for at in strips(extent):
        im = slice(extent + at.start, extent + at.stop)
        hr, hi = hs_ref[at], hs_ref[im]
        for b in range(blocks):
            dr, di = d_ref[b, at], d_ref[b, im]
            put_halves(dr * hr + di * hi, high_r.at[b], low_r.at[b], at)
            put_halves(di * hr - dr * hi, high_r.at[b], low_r.at[b], im)
    for b in range(blocks):
        r_ref[b] = product(inverse_ref[...], stacked_rows(high_r.at[b], low_r.at[b]))
    w = [-w_ref[i : i + 1] for i in range(taps)]
    gate = [gate_ref[i : i + 1] for i in range(taps)]
    nothing = jnp.zeros((STRIP, width), F32)
    after_r = after_dq = nothing[:8]
    for row in range(rows - STRIP, -lead - 1, -STRIP):
        block, at = (row + extent) // extent, (row + extent) % extent
        if row < -extent:
            r = nothing
        elif block == 0:
            r = r_ref[0, at : at + STRIP]
        elif block == blocks:
            r = r_ref[blocks - 1, extent + at : extent + at + STRIP]
        else:
            r = r_ref[block - 1, extent + at : extent + at + STRIP] + r_ref[block, at : at + STRIP]
        total = w[0] * r
        for i in range(1, taps):
            total = total + w[i] * advanced(r, after_r, i)
        after_r = r[:8]
        if row >= -STRIP:
            dq = dq_ref[row : row + STRIP] if row >= 0 else nothing
            if row >= 0:
                total = total + gate[0] * dq
            for i in range(1, taps):
                total = total + gate[i] * advanced(dq, after_dq, i)
            after_dq = dq[:8]
        if row < 0:
            head_ref[lead + row : lead + row + STRIP] = total.astype(BF16)
        elif row < rows - lead:
            grad_ref[row : row + STRIP] = total.astype(BF16)
        else:
            end_ref[row - rows + lead : row - rows + lead + STRIP] = total


IN_VMEM = pl.BlockSpec(memory_space=pltpu.VMEM)
IN_SMEM = pl.BlockSpec(memory_space=pltpu.SMEM)
ANYWHERE = pl.BlockSpec(memory_space=pl.ANY)


def place_of(me_ref, k, pieces, piece):
    return pl.ds(pl.multiple_of(lax.rem(me_ref[0] + (pieces - k), pieces) * piece, piece), piece)


def call(name, body, inputs, constants, outs, scratch, block, cost, me, pieces=(), kept_outs=(), at_end=None):
    moved = [isinstance(x, list) for x in inputs]
    arrays = [x[0] if isinstance(x, list) else x for x in inputs]
    width = arrays[0].shape[-1]
    blocks = width // block
    last_outs = () if at_end is None else at_end[0]
    n_pieces, n_in, n_const = len(pieces), len(arrays), len(constants)
    n_out = len(outs) + len(last_outs)
    held = [x for x, move in zip(arrays, moved) if move] + list(constants) + list(kept_outs)
    if pieces:
        held.append(jax.ShapeDtypeStruct((n_pieces * pieces[0].shape[0], width), pieces[0].dtype))

    def kernel(*refs):
        me_ref, piece_refs, refs = refs[0], refs[1 : 1 + n_pieces], refs[1 + n_pieces :]
        given, refs = refs[: n_in + n_const], refs[n_in + n_const :]
        results, refs = refs[:n_out], refs[n_out:]
        temporary, kept, sems, const_sems = refs[: len(scratch)], list(refs[len(scratch) : -2]), *refs[-2:]
        ins, sources = [], []
        for ref, move in zip(given, moved):
            ins.append(kept.pop(0) if move else ref)
            if move:
                sources.append((ref, ins[-1]))
        whole = [kept.pop(0) for _ in range(n_const)]
        stay = [kept.pop(0) for _ in kept_outs]
        if pieces:
            ins.insert(0, kept.pop(0))
            sources += [
                (ref, ins[0].at[place_of(me_ref, k, n_pieces, ref.shape[0])]) for k, ref in enumerate(piece_refs)
            ]

        def cut(ref, j):
            place = pl.ds(pl.multiple_of(j * block, block), block)
            return ref.at[(slice(None),) * (len(ref.shape) - 1) + (place,)]

        def copies(j):
            return [pltpu.make_async_copy(cut(a, j), cut(b, j), sems.at[i, j]) for i, (a, b) in enumerate(sources)]

        constant_copies = [
            pltpu.make_async_copy(a, b, const_sems.at[i]) for i, (a, b) in enumerate(zip(given[n_in:], whole))
        ]
        for copy in constant_copies:
            copy.start()
        for j in range(blocks):
            for copy in copies(j):
                copy.start()
        for copy in constant_copies:
            copy.wait()

        def one(j):
            for copy in copies(j):
                copy.wait()
            shown = list(results[: len(outs)]) + stay
            body(*[cut(x, j) for x in ins], *whole, *[cut(x, j) for x in shown], *temporary)

        pl.loop(0, blocks)(one)
        if at_end is not None:
            at_end[1](me_ref, stay, results[len(outs) :])

    return pl.pallas_call(
        kernel,
        in_specs=[IN_SMEM]
        + [ANYWHERE] * n_pieces
        + [ANYWHERE if move else IN_VMEM for move in moved]
        + [ANYWHERE] * n_const,
        out_specs=[IN_VMEM] * n_out,
        scratch_shapes=[pltpu.VMEM(shape, dtype) for shape, dtype in scratch]
        + [pltpu.VMEM(x.shape, x.dtype) for x in held]
        + [
            pltpu.SemaphoreType.DMA((n_pieces + sum(moved) + 1, blocks)),
            pltpu.SemaphoreType.DMA((n_const,)),
        ],
        out_shape=[*outs, *last_outs],
        compiler_params=pltpu.CompilerParams(vmem_limit_bytes=VMEM_LIMIT),
        cost_estimate=cost,
        name=name,
    )(me, *pieces, *arrays, *constants)


def tail_step(pieces, me, lead):
    piece, width = pieces[0].shape
    rows = piece * len(pieces)

    def kernel(me_ref, *refs):
        tail_ref, held, sems, sem = refs[len(pieces) :]
        copies = [
            pltpu.make_async_copy(ref, held.at[place_of(me_ref, k, len(pieces), piece)], sems.at[k])
            for k, ref in enumerate(refs[: len(pieces)])
        ]
        for copy in copies:
            copy.start()
        for copy in copies:
            copy.wait()
        out = pltpu.make_async_copy(held.at[pl.ds(rows - lead, lead), :], tail_ref, sem)
        out.start()
        out.wait()

    return pl.pallas_call(
        kernel,
        in_specs=[IN_SMEM] + [ANYWHERE] * len(pieces),
        out_specs=ANYWHERE,
        scratch_shapes=[
            pltpu.VMEM((rows, width), BF16),
            pltpu.SemaphoreType.DMA((len(pieces),)),
            pltpu.SemaphoreType.DMA,
        ],
        out_shape=jax.ShapeDtypeStruct((lead, width), BF16),
        compiler_params=pltpu.CompilerParams(vmem_limit_bytes=VMEM_LIMIT),
        cost_estimate=BRIEF,
        name="tail_step",
    )(me, *pieces)


def signal_step(u_pieces, me, halo, h, w, matrices, block):
    width = h.shape[1]
    rows, extent = u_pieces[0].shape[0] * len(u_pieces), h.shape[0]
    blocks = rows // extent
    outs = [
        jax.ShapeDtypeStruct((blocks, 2 * extent, width), F32),
        jax.ShapeDtypeStruct((2 * extent, width), F32),
        jax.ShapeDtypeStruct((rows, width), F32),
        jax.ShapeDtypeStruct((rows, width), BF16),
    ]
    scratch = [((extent, block), BF16)] * 2 + [((blocks, 2 * extent, block), BF16)] * 2
    scratch += [((STRIP + rows, block), F32)]
    constants = [matrices[name] for name in ("both", "short", "around")]

    def body(u_ref, *refs):
        refs[9][...] = u_ref[...]
        signal_kernel(u_ref, *refs[:9], *refs[10:])

    return call(
        "signal_step", body, [[halo], [h], [w]], constants, outs, scratch, block, BRIEF, me, u_pieces
    )


def gradient_step(g_pieces, me, u, halo, h, us, hs, z, gate, w, matrices, scale, block, shares):
    rows, width = u.shape
    extent, taps, lead = h.shape[0], gate.shape[0], halo.shape[0]
    blocks = rows // extent
    count, part = extent + -(-2 * taps // 16) * 16, width // shares
    outs = [
        jax.ShapeDtypeStruct((rows - lead, width), BF16),
        jax.ShapeDtypeStruct((lead, width), F32),
        jax.ShapeDtypeStruct((lead, width), BF16),
    ]
    sums = [jax.ShapeDtypeStruct((count, width), F32)]
    spectra = (blocks, 2 * extent, block)
    scratch = [(spectra, F32), ((rows, block), F32)]
    scratch += [((rows, block), BF16)] * 2 + [((2 * extent, block), BF16)] * 2
    scratch += [(spectra, BF16)] * 2 + [(spectra, F32)]
    ends = [jax.ShapeDtypeStruct((count, part), BF16 if k else F32) for k in range(shares)]

    def body(g, u, halo, h, us, hs, z, gate, w, short, inverse, grad, end, head, sums, d, dq, *temporary):
        sums_kernel(scale, g, u, halo, h, us, z, gate, w, short, inverse, d, dq, sums, *temporary[:4])
        input_kernel(lead, d, dq, hs, gate, w, inverse, grad, end, head, *temporary[4:])

    def share(me_ref, kept, refs):
        for k, ref in enumerate(refs):
            start = pl.multiple_of((me_ref[1] ^ k) * part, part) if shares > 1 else 0
            ref[...] = kept[0][:, pl.ds(start, part)].astype(ref.dtype)

    main, end, head, *terms = call(
        "gradient_step", body, [u, [halo], [h], us, hs, z, [gate], [w]],
        [matrices[name] for name in ("short", "inverse")], outs, scratch, block, LONG, me, g_pieces, sums,
        (ends, share),
    )
    return main, end, head, terms


def slices(x, axis, start, part):
    count = lax.axis_size(axis)
    me = lax.axis_index(axis)
    width = x.shape[1] // count
    return [
        lax.dynamic_slice_in_dim(x, lax.rem(me + k, count) * width + start, part, axis=1)
        for k in range(count)
    ]


def exchange(pieces, axis):
    count = lax.axis_size(axis)
    got = [pieces[0]] + [None] * (count - 1)
    for k in sorted(range(1, count), key=lambda k: abs(2 * k - count)):
        got[k] = lax.ppermute(pieces[k], axis, [(i, (i + k) % count) for i in range(count)])
    return got


def shifted(x, axis, by):
    count = lax.axis_size(axis)
    pairs = [(i, i + by) for i in range(count) if 0 <= i + by < count]
    return lax.ppermute(x, axis, pairs)


def at_once(exchange_of, x, axis):
    return lax.cond(lax.axis_index(axis) >= 0, exchange_of, jnp.zeros_like, x)


def partner(x, axis, bit):
    count = lax.axis_size(axis)
    return lax.ppermute(x, axis, [(i, i ^ bit) for i in range(count)])


def summed(x, axis):
    total, bit, count = x + partner(x, axis, 1), 2, lax.axis_size(axis)
    while bit < count:
        short = total.astype(BF16)
        total = short.astype(F32) + partner(short, axis, bit).astype(F32)
        bit *= 2
    return total


def finish_step(terms, me, sizes):
    part, shares = terms[0].shape[1], len(terms)
    width = part * shares

    def kernel(me_ref, *refs):
        terms, outs, held, sems = refs[:shares], refs[shares : shares + len(sizes)], refs[shares + len(sizes) : -1], refs[-1]
        copies = []
        for k, term in enumerate(terms):
            place = pl.ds(pl.multiple_of((me_ref[1] ^ k) * part, part), part)
            x, row = term[...].astype(F32), 0
            for i, (size, out, ref) in enumerate(zip(sizes, outs, held)):
                ref[:, place] = x[row : row + size]
                row += size
                copies.append(pltpu.make_async_copy(ref.at[:, place], out.at[:, place], sems.at[i, k]))
                copies[-1].start()
        for copy in copies:
            copy.wait()

    return pl.pallas_call(
        kernel,
        in_specs=[IN_SMEM] + [IN_VMEM] * shares,
        out_specs=[ANYWHERE] * len(sizes),
        scratch_shapes=[pltpu.VMEM((size, width), F32) for size in sizes]
        + [pltpu.SemaphoreType.DMA((len(sizes), shares))],
        out_shape=[jax.ShapeDtypeStruct((size, width), F32) for size in sizes],
        compiler_params=pltpu.CompilerParams(vmem_limit_bytes=VMEM_LIMIT),
        cost_estimate=BRIEF,
        name="finish_step",
    )(me, *terms)


def shards(out_grad, saved_input, explicit_filter_weights, gate_taps, value_featurizer_weights):
    extent, width = explicit_filter_weights.shape
    taps = gate_taps.shape[0]
    me = jnp.stack([lax.axis_index("tp"), lax.axis_index("ctx") // 2]).astype(jnp.int32)
    rows = out_grad.shape[0] * lax.axis_size("tp")
    lead = -(-(extent + taps - 2) // 16) * 16
    block = min(BLOCK, width)
    matrices = {name: jnp.asarray(m) for name, m in transforms(extent).items()}
    scale = 1.0 / math.sqrt(rows * lax.axis_size("ctx"))
    h, gate, w = explicit_filter_weights, gate_taps, value_featurizer_weights
    u_pieces = exchange(slices(saved_input, "tp", 0, width), "tp")
    g_slices = slices(out_grad, "tp", 0, width)
    u_pieces, g_slices = lax.optimization_barrier((u_pieces, g_slices))
    g_pieces = exchange(g_slices, "tp")
    tail = tail_step(u_pieces, me, lead)
    halo = at_once(lambda x: shifted(x, "ctx", 1), tail, "ctx")
    us, hs, z, u = signal_step(u_pieces, me, halo, h, w, matrices, block)
    chips = lax.axis_size("ctx") // 2
    shares = chips if chips == 4 and width % (128 * chips) == 0 else 1
    main, end, head, terms = gradient_step(
        g_pieces, me, u, halo, h, us, hs, z, gate, w, matrices, scale, block, shares
    )
    sizes = (extent, taps, taps)
    if shares > 1:
        terms = [terms[0]] + [partner(terms[k], "ctx", 2 * k).astype(F32) for k in range(1, shares)]
        incoming = shifted(head, "ctx", -1)
        while len(terms) > 1:
            terms = [a + b for a, b in zip(terms[::2], terms[1::2])]
        total = terms[0] + partner(terms[0], "ctx", 1)
        total, incoming = lax.optimization_barrier((total, incoming))
        total = total.astype(BF16)
        terms = [total] + [partner(total, "ctx", 2 * k) for k in range(1, shares)]
        sums = finish_step(terms, me, sizes)
    else:
        incoming = shifted(head, "ctx", -1)
        total = summed(terms[0], "ctx")
        ends = np.cumsum(sizes)
        sums = [total[stop - size : stop] for size, stop in zip(sizes, ends)]
    end = (end + incoming.astype(F32)).astype(BF16)
    return (jnp.concatenate([main, end], axis=0), *sums)


def solution(mesh):
    placed = (
        P(("ctx", "tp"), None),
        P(("ctx", "tp"), None),
        P(None, "tp"),
        P(None, "tp"),
        P(None, "tp"),
    )
    return jax.shard_map(
        shards,
        mesh=mesh,
        in_specs=placed,
        out_specs=(P("ctx", "tp"), P(None, "tp"), P(None, "tp"), P(None, "tp")),
        check_vma=False,
    )
```

```python
import math

import jax
import jax.numpy as jnp
import numpy as np
from jax import lax
from jax.experimental import pallas as pl
from jax.experimental.pallas import tpu as pltpu
from jax.sharding import PartitionSpec as P

F32 = jnp.float32
BF16 = jnp.bfloat16
VMEM_LIMIT = 16 * 1024 * 1024
BLOCK = 1024
BRIEF = pl.CostEstimate(flops=1000, bytes_accessed=1000, transcendentals=0)
LONG = pl.CostEstimate(flops=20_000_000_000, bytes_accessed=100_000_000, transcendentals=0)


STRIP = 16


def strips(rows):
    return [slice(i, i + STRIP) for i in range(0, rows, STRIP)]


def put_halves(x, high_ref, low_ref, rows):
    high = x.astype(BF16)
    high_ref[rows] = high
    low_ref[rows] = (x - high.astype(F32)).astype(BF16)


def stacked_rows(high_ref, low_ref, rows=slice(None)):
    high = high_ref[rows]
    return jnp.concatenate([high, high, low_ref[rows]], axis=0)


def product(matrix, x):
    return jnp.dot(matrix, x, preferred_element_type=F32)


def transforms(extent):
    points = 2 * extent
    angle = np.pi * np.outer(2 * np.arange(extent) + 1, np.arange(points)) / points
    whole = np.concatenate([np.cos(angle), -np.sin(angle)])
    back = whole.T / extent

    def split(matrix, terms=3):
        high = matrix.astype(jnp.bfloat16)
        low = (matrix - high.astype(np.float64)).astype(jnp.bfloat16)
        return np.concatenate([high, low, high][:terms], axis=1)

    return {
        "both": split(whole, 2),
        "short": split(whole[:, :extent]),
        "inverse": split(np.concatenate([-back[extent:], back[:extent]])),
        "around": split(-back[extent - STRIP :]),
    }


def delayed(before, x, by):
    return pltpu.roll(jnp.concatenate([before, x], axis=0), by, 0)[8:]


def advanced(x, after, by):
    both = jnp.concatenate([x, after], axis=0)
    return pltpu.roll(both, both.shape[0] - by, 0)[: x.shape[0]]


def folded(x):
    return sum(x[i : i + 8] for i in range(8, x.shape[0], 8)) + x[:8]


def filtered(u, before, taps):
    value = taps[0] * u
    for j in range(1, len(taps)):
        value = value + taps[j] * delayed(before, u, j)
    return value


def convolved(matrix, spectrum, hs_ref, high_ref, low_ref):
    for at in strips(hs_ref.shape[0] // 2):
        im = slice(at.start + hs_ref.shape[0] // 2, at.stop + hs_ref.shape[0] // 2)
        ur, ui, hr, hi = spectrum[at], spectrum[im], hs_ref[at], hs_ref[im]
        put_halves(ur * hr - ui * hi, high_ref, low_ref, at)
        put_halves(ur * hi + ui * hr, high_ref, low_ref, im)
    return product(matrix, stacked_rows(high_ref, low_ref))


def twice(x):
    return jnp.concatenate([x, x], axis=0)


def signal_kernel(
    u_ref, halo_ref, h_ref, w_ref, both_ref, short_ref, around_ref, us_ref, hs_ref, z_ref, *scratch
):
    high_h, low_h, high_p, low_p, p_ref = scratch
    extent = h_ref.shape[0]
    lead, width = halo_ref.shape
    blocks = us_ref.shape[0]
    for at in strips(extent):
        put_halves(-h_ref[at], high_h, low_h, at)
    hs_ref[...] = product(short_ref[...], stacked_rows(high_h, low_h))
    for b in range(blocks):
        last = u_ref[b * extent : (b + 1) * extent]
        first = halo_ref[lead - extent :] if b == 0 else u_ref[(b - 1) * extent : b * extent]
        us_ref[b] = product(both_ref[...], jnp.concatenate([first, last] * 2, axis=0))
    for b in range(blocks):
        matrix = around_ref[...] if b == 0 else around_ref[STRIP:]
        rows = slice(0 if b == 0 else STRIP + b * extent, STRIP + (b + 1) * extent)
        p_ref[rows] = convolved(matrix, us_ref.at[b], hs_ref, high_p.at[b], low_p.at[b])
    ahead = halo_ref[lead - extent - STRIP : lead - extent].astype(F32)[STRIP - 1 :]
    final = u_ref[extent - STRIP : extent].astype(F32)[STRIP - 1 :]
    mend = h_ref[extent - 1 : extent] * (ahead + final)
    at_second = lax.broadcasted_iota(jnp.int32, (8, width), 0) == 6
    before = p_ref[8:STRIP] + jnp.where(at_second, mend, 0.0)
    w = [w_ref[i : i + 1] for i in range(w_ref.shape[0])]
    for at in strips(z_ref.shape[0]):
        p = p_ref[STRIP + at.start : STRIP + at.stop]
        z_ref[at] = filtered(p, before, w)
        before = p[-8:]


def sums_kernel(
    scale, g_ref, u_ref, halo_ref, h_ref, us_ref, z_ref, gate_ref, w_ref, short_ref, inverse_ref,
    d_ref, dq_ref, sums_ref, *scratch
):
    high_d, low_d, high_c, low_c = scratch
    extent = h_ref.shape[0]
    rows, width = u_ref.shape
    taps = gate_ref.shape[0]
    blocks = rows // extent
    gate = [gate_ref[i : i + 1] for i in range(taps)]
    w = [w_ref[i : i + 1] for i in range(taps)]
    gate_sums = [jnp.zeros((8, width), F32) for _ in range(taps)]
    ahead = halo_ref[halo_ref.shape[0] - STRIP :].astype(F32)
    before = ahead[8:]
    first = halo_ref[halo_ref.shape[0] - extent - STRIP : halo_ref.shape[0] - extent].astype(F32)
    preceding = [first[STRIP - 1 :], ahead[STRIP - 1 :]]
    mend = None
    for at in strips(rows):
        g, u = g_ref[at].astype(F32), u_ref[at].astype(F32)
        late = [u] + [delayed(before, u, i) for i in range(1, taps)]
        before = u[8:]
        q = gate[0] * u
        for i in range(1, taps):
            q = q + gate[i] * late[i]
        dz, dq = g * q, g * z_ref[at]
        dq_ref[at] = dq
        put_halves(dz, high_d, low_d, at)
        gate_sums = [total + folded(dq * x) for total, x in zip(gate_sums, late)]
        if at.start % extent == 0:
            b, start = at.start // extent, dz[:1]
            if b >= 2:
                preceding.append(u_ref[(b - 1) * extent - STRIP : (b - 1) * extent].astype(F32)[STRIP - 1 :])
        if at.stop % extent == 0:
            term = start * (u[STRIP - 1 :] + preceding[b])
            mend = term if mend is None else mend + term
    for b in range(blocks):
        window = slice(b * extent, (b + 1) * extent)
        d_ref[b] = product(short_ref[...], stacked_rows(high_d, low_d, window))
    for at in strips(extent):
        im = slice(extent + at.start, extent + at.stop)
        cr = ci = None
        for b in range(blocks):
            dr, di, ur, ui = d_ref[b, at], d_ref[b, im], us_ref[b, at], us_ref[b, im]
            real, imaginary = dr * ur + di * ui, di * ur - dr * ui
            cr, ci = (real, imaginary) if cr is None else (cr + real, ci + imaginary)
        put_halves(cr, high_c, low_c, at)
        put_halves(ci, high_c, low_c, im)
    lags = product(inverse_ref[: extent + STRIP], stacked_rows(high_c, low_c)) * scale
    at_last = lax.broadcasted_iota(jnp.int32, (8, width), 0) == 1
    after = lags[extent : extent + 8] + jnp.where(at_last, mend * scale, 0.0)
    value_sums = [jnp.zeros((8, width), F32) for _ in range(taps)]
    for row in range(extent - STRIP, -1, -STRIP):
        c = lags[row : row + STRIP]
        early = [c] + [advanced(c, after, i) for i in range(1, taps)]
        after = c[:8]
        total = w[0] * c
        for i in range(1, taps):
            total = total + w[i] * early[i]
        sums_ref[row : row + STRIP] = total
        h = h_ref[row : row + STRIP]
        value_sums = [sums + folded(h * x) for sums, x in zip(value_sums, early)]
    rest = [jnp.sum(x, axis=0, keepdims=True) * scale for x in gate_sums]
    rest += [jnp.sum(x, axis=0, keepdims=True) for x in value_sums]
    spare = sums_ref.shape[0] - extent - 2 * taps
    rest.append(jnp.zeros((spare, width), F32))
    sums_ref[extent:] = jnp.concatenate(rest, axis=0)


def input_kernel(
    lead, d_ref, dq_ref, hs_ref, gate_ref, w_ref, inverse_ref, grad_ref, end_ref, head_ref, *scratch
):
    high_r, low_r, r_ref = scratch
    extent = hs_ref.shape[0] // 2
    rows, width = dq_ref.shape
    taps = gate_ref.shape[0]
    blocks = rows // extent
    for at in strips(extent):
        im = slice(extent + at.start, extent + at.stop)
        hr, hi = hs_ref[at], hs_ref[im]
        for b in range(blocks):
            dr, di = d_ref[b, at], d_ref[b, im]
            put_halves(dr * hr + di * hi, high_r.at[b], low_r.at[b], at)
            put_halves(di * hr - dr * hi, high_r.at[b], low_r.at[b], im)
    for b in range(blocks):
        r_ref[b] = product(inverse_ref[...], stacked_rows(high_r.at[b], low_r.at[b]))
    w = [-w_ref[i : i + 1] for i in range(taps)]
    gate = [gate_ref[i : i + 1] for i in range(taps)]
    nothing = jnp.zeros((STRIP, width), F32)
    after_r = after_dq = nothing[:8]
    for row in range(rows - STRIP, -lead - 1, -STRIP):
        block, at = (row + extent) // extent, (row + extent) % extent
        if row < -extent:
            r = nothing
        elif block == 0:
            r = r_ref[0, at : at + STRIP]
        elif block == blocks:
            r = r_ref[blocks - 1, extent + at : extent + at + STRIP]
        else:
            r = r_ref[block - 1, extent + at : extent + at + STRIP] + r_ref[block, at : at + STRIP]
        total = w[0] * r
        for i in range(1, taps):
            total = total + w[i] * advanced(r, after_r, i)
        after_r = r[:8]
        if row >= -STRIP:
            dq = dq_ref[row : row + STRIP] if row >= 0 else nothing
            if row >= 0:
                total = total + gate[0] * dq
            for i in range(1, taps):
                total = total + gate[i] * advanced(dq, after_dq, i)
            after_dq = dq[:8]
        if row < 0:
            head_ref[lead + row : lead + row + STRIP] = total.astype(BF16)
        elif row < rows - lead:
            grad_ref[row : row + STRIP] = total.astype(BF16)
        else:
            end_ref[row - rows + lead : row - rows + lead + STRIP] = total


IN_VMEM = pl.BlockSpec(memory_space=pltpu.VMEM)
IN_SMEM = pl.BlockSpec(memory_space=pltpu.SMEM)
ANYWHERE = pl.BlockSpec(memory_space=pl.ANY)


def place_of(me_ref, k, pieces, piece):
    return pl.ds(pl.multiple_of(lax.rem(me_ref[0] + (pieces - k), pieces) * piece, piece), piece)


def call(name, body, inputs, constants, outs, scratch, block, cost, me, pieces=(), kept_outs=(), at_end=None):
    moved = [isinstance(x, list) for x in inputs]
    arrays = [x[0] if isinstance(x, list) else x for x in inputs]
    width = arrays[0].shape[-1]
    blocks = width // block
    last_outs = () if at_end is None else at_end[0]
    n_pieces, n_in, n_const = len(pieces), len(arrays), len(constants)
    n_out = len(outs) + len(last_outs)
    held = [x for x, move in zip(arrays, moved) if move] + list(constants) + list(kept_outs)
    if pieces:
        held.append(jax.ShapeDtypeStruct((n_pieces * pieces[0].shape[0], width), pieces[0].dtype))

    def kernel(*refs):
        me_ref, piece_refs, refs = refs[0], refs[1 : 1 + n_pieces], refs[1 + n_pieces :]
        given, refs = refs[: n_in + n_const], refs[n_in + n_const :]
        results, refs = refs[:n_out], refs[n_out:]
        temporary, kept, sems, const_sems = refs[: len(scratch)], list(refs[len(scratch) : -2]), *refs[-2:]
        ins, sources = [], []
        for ref, move in zip(given, moved):
            ins.append(kept.pop(0) if move else ref)
            if move:
                sources.append((ref, ins[-1]))
        whole = [kept.pop(0) for _ in range(n_const)]
        stay = [kept.pop(0) for _ in kept_outs]
        if pieces:
            ins.insert(0, kept.pop(0))
            sources += [
                (ref, ins[0].at[place_of(me_ref, k, n_pieces, ref.shape[0])]) for k, ref in enumerate(piece_refs)
            ]

        def cut(ref, j):
            place = pl.ds(pl.multiple_of(j * block, block), block)
            return ref.at[(slice(None),) * (len(ref.shape) - 1) + (place,)]

        def copies(j):
            return [pltpu.make_async_copy(cut(a, j), cut(b, j), sems.at[i, j]) for i, (a, b) in enumerate(sources)]

        constant_copies = [
            pltpu.make_async_copy(a, b, const_sems.at[i]) for i, (a, b) in enumerate(zip(given[n_in:], whole))
        ]
        for copy in constant_copies:
            copy.start()
        for j in range(blocks):
            for copy in copies(j):
                copy.start()
        for copy in constant_copies:
            copy.wait()

        def one(j):
            for copy in copies(j):
                copy.wait()
            shown = list(results[: len(outs)]) + stay
            body(*[cut(x, j) for x in ins], *whole, *[cut(x, j) for x in shown], *temporary)

        pl.loop(0, blocks)(one)
        if at_end is not None:
            at_end[1](me_ref, stay, results[len(outs) :])

    return pl.pallas_call(
        kernel,
        in_specs=[IN_SMEM]
        + [ANYWHERE] * n_pieces
        + [ANYWHERE if move else IN_VMEM for move in moved]
        + [ANYWHERE] * n_const,
        out_specs=[IN_VMEM] * n_out,
        scratch_shapes=[pltpu.VMEM(shape, dtype) for shape, dtype in scratch]
        + [pltpu.VMEM(x.shape, x.dtype) for x in held]
        + [
            pltpu.SemaphoreType.DMA((n_pieces + sum(moved) + 1, blocks)),
            pltpu.SemaphoreType.DMA((n_const,)),
        ],
        out_shape=[*outs, *last_outs],
        compiler_params=pltpu.CompilerParams(vmem_limit_bytes=VMEM_LIMIT),
        cost_estimate=cost,
        name=name,
    )(me, *pieces, *arrays, *constants)


def tail_step(pieces, me, lead):
    piece, width = pieces[0].shape
    rows = piece * len(pieces)

    def kernel(me_ref, *refs):
        tail_ref, held, sems, sem = refs[len(pieces) :]
        copies = [
            pltpu.make_async_copy(ref, held.at[place_of(me_ref, k, len(pieces), piece)], sems.at[k])
            for k, ref in enumerate(refs[: len(pieces)])
        ]
        for copy in copies:
            copy.start()
        for copy in copies:
            copy.wait()
        out = pltpu.make_async_copy(held.at[pl.ds(rows - lead, lead), :], tail_ref, sem)
        out.start()
        out.wait()

    return pl.pallas_call(
        kernel,
        in_specs=[IN_SMEM] + [ANYWHERE] * len(pieces),
        out_specs=ANYWHERE,
        scratch_shapes=[
            pltpu.VMEM((rows, width), BF16),
            pltpu.SemaphoreType.DMA((len(pieces),)),
            pltpu.SemaphoreType.DMA,
        ],
        out_shape=jax.ShapeDtypeStruct((lead, width), BF16),
        compiler_params=pltpu.CompilerParams(vmem_limit_bytes=VMEM_LIMIT),
        cost_estimate=BRIEF,
        name="tail_step",
    )(me, *pieces)


def signal_step(u_pieces, me, halo, h, w, matrices, block):
    width = h.shape[1]
    rows, extent = u_pieces[0].shape[0] * len(u_pieces), h.shape[0]
    blocks = rows // extent
    outs = [
        jax.ShapeDtypeStruct((blocks, 2 * extent, width), F32),
        jax.ShapeDtypeStruct((2 * extent, width), F32),
        jax.ShapeDtypeStruct((rows, width), F32),
        jax.ShapeDtypeStruct((rows, width), BF16),
    ]
    scratch = [((extent, block), BF16)] * 2 + [((blocks, 2 * extent, block), BF16)] * 2
    scratch += [((STRIP + rows, block), F32)]
    constants = [matrices[name] for name in ("both", "short", "around")]

    def body(u_ref, *refs):
        refs[9][...] = u_ref[...]
        signal_kernel(u_ref, *refs[:9], *refs[10:])

    return call(
        "signal_step", body, [[halo], [h], [w]], constants, outs, scratch, block, BRIEF, me, u_pieces
    )


def gradient_step(g_pieces, me, u, halo, h, us, hs, z, gate, w, matrices, scale, block, shares):
    rows, width = u.shape
    extent, taps, lead = h.shape[0], gate.shape[0], halo.shape[0]
    blocks = rows // extent
    count, part = extent + -(-2 * taps // 16) * 16, width // shares
    outs = [
        jax.ShapeDtypeStruct((rows - lead, width), BF16),
        jax.ShapeDtypeStruct((lead, width), F32),
        jax.ShapeDtypeStruct((lead, width), BF16),
    ]
    sums = [jax.ShapeDtypeStruct((count, width), F32)]
    spectra = (blocks, 2 * extent, block)
    scratch = [(spectra, F32), ((rows, block), F32)]
    scratch += [((rows, block), BF16)] * 2 + [((2 * extent, block), BF16)] * 2
    scratch += [(spectra, BF16)] * 2 + [(spectra, F32)]
    ends = [jax.ShapeDtypeStruct((count, part), BF16 if k else F32) for k in range(shares)]

    def body(g, u, halo, h, us, hs, z, gate, w, short, inverse, grad, end, head, sums, d, dq, *temporary):
        sums_kernel(scale, g, u, halo, h, us, z, gate, w, short, inverse, d, dq, sums, *temporary[:4])
        input_kernel(lead, d, dq, hs, gate, w, inverse, grad, end, head, *temporary[4:])

    def share(me_ref, kept, refs):
        for k, ref in enumerate(refs):
            start = pl.multiple_of((me_ref[1] ^ k) * part, part) if shares > 1 else 0
            ref[...] = kept[0][:, pl.ds(start, part)].astype(ref.dtype)

    main, end, head, *terms = call(
        "gradient_step", body, [u, [halo], [h], us, hs, z, [gate], [w]],
        [matrices[name] for name in ("short", "inverse")], outs, scratch, block, LONG, me, g_pieces, sums,
        (ends, share),
    )
    return main, end, head, terms


def slices(x, axis, start, part):
    count = lax.axis_size(axis)
    me = lax.axis_index(axis)
    width = x.shape[1] // count
    return [
        lax.dynamic_slice_in_dim(x, lax.rem(me + k, count) * width + start, part, axis=1)
        for k in range(count)
    ]


def exchange(pieces, axis):
    count = lax.axis_size(axis)
    got = [pieces[0]] + [None] * (count - 1)
    for k in sorted(range(1, count), key=lambda k: -abs(2 * k - count)):
        got[k] = lax.ppermute(pieces[k], axis, [(i, (i + k) % count) for i in range(count)])
    return got


def shifted(x, axis, by):
    count = lax.axis_size(axis)
    pairs = [(i, i + by) for i in range(count) if 0 <= i + by < count]
    return lax.ppermute(x, axis, pairs)


def at_once(exchange_of, x, axis):
    return lax.cond(lax.axis_index(axis) >= 0, exchange_of, jnp.zeros_like, x)


def partner(x, axis, bit):
    count = lax.axis_size(axis)
    return lax.ppermute(x, axis, [(i, i ^ bit) for i in range(count)])


def summed(x, axis):
    total, bit, count = x + partner(x, axis, 1), 2, lax.axis_size(axis)
    while bit < count:
        short = total.astype(BF16)
        total = short.astype(F32) + partner(short, axis, bit).astype(F32)
        bit *= 2
    return total


def finish_step(terms, me, sizes):
    part, shares = terms[0].shape[1], len(terms)
    width = part * shares

    def kernel(me_ref, *refs):
        terms, outs, held, sems = refs[:shares], refs[shares : shares + len(sizes)], refs[shares + len(sizes) : -1], refs[-1]
        copies = []
        for k, term in enumerate(terms):
            place = pl.ds(pl.multiple_of((me_ref[1] ^ k) * part, part), part)
            x, row = term[...].astype(F32), 0
            for i, (size, out, ref) in enumerate(zip(sizes, outs, held)):
                ref[:, place] = x[row : row + size]
                row += size
                copies.append(pltpu.make_async_copy(ref.at[:, place], out.at[:, place], sems.at[i, k]))
                copies[-1].start()
        for copy in copies:
            copy.wait()

    return pl.pallas_call(
        kernel,
        in_specs=[IN_SMEM] + [IN_VMEM] * shares,
        out_specs=[ANYWHERE] * len(sizes),
        scratch_shapes=[pltpu.VMEM((size, width), F32) for size in sizes]
        + [pltpu.SemaphoreType.DMA((len(sizes), shares))],
        out_shape=[jax.ShapeDtypeStruct((size, width), F32) for size in sizes],
        compiler_params=pltpu.CompilerParams(vmem_limit_bytes=VMEM_LIMIT),
        cost_estimate=BRIEF,
        name="finish_step",
    )(me, *terms)


def shards(out_grad, saved_input, explicit_filter_weights, gate_taps, value_featurizer_weights):
    extent, width = explicit_filter_weights.shape
    taps = gate_taps.shape[0]
    me = jnp.stack([lax.axis_index("tp"), lax.axis_index("ctx") // 2]).astype(jnp.int32)
    rows = out_grad.shape[0] * lax.axis_size("tp")
    lead = -(-(extent + taps - 2) // 16) * 16
    block = min(BLOCK, width)
    matrices = {name: jnp.asarray(m) for name, m in transforms(extent).items()}
    scale = 1.0 / math.sqrt(rows * lax.axis_size("ctx"))
    h, gate, w = explicit_filter_weights, gate_taps, value_featurizer_weights
    u_pieces = exchange(slices(saved_input, "tp", 0, width), "tp")
    g_slices = slices(out_grad, "tp", 0, width)
    u_pieces, g_slices = lax.optimization_barrier((u_pieces, g_slices))
    g_pieces = exchange(g_slices, "tp")
    tail = tail_step(u_pieces, me, lead)
    halo = at_once(lambda x: shifted(x, "ctx", 1), tail, "ctx")
    us, hs, z, u = signal_step(u_pieces, me, halo, h, w, matrices, block)
    chips = lax.axis_size("ctx") // 2
    shares = chips if chips == 4 and width % (128 * chips) == 0 else 1
    main, end, head, terms = gradient_step(
        g_pieces, me, u, halo, h, us, hs, z, gate, w, matrices, scale, block, shares
    )
    sizes = (extent, taps, taps)
    if shares > 1:
        terms = [terms[0]] + [partner(terms[k], "ctx", 2 * k).astype(F32) for k in range(1, shares)]
        incoming = shifted(head, "ctx", -1)
        while len(terms) > 1:
            terms = [a + b for a, b in zip(terms[::2], terms[1::2])]
        total = terms[0] + partner(terms[0], "ctx", 1)
        total, incoming = lax.optimization_barrier((total, incoming))
        total = total.astype(BF16)
        terms = [total] + [partner(total, "ctx", 2 * k) for k in range(1, shares)]
        sums = finish_step(terms, me, sizes)
    else:
        incoming = shifted(head, "ctx", -1)
        total = summed(terms[0], "ctx")
        ends = np.cumsum(sizes)
        sums = [total[stop - size : stop] for size, stop in zip(sizes, ends)]
    end = (end + incoming.astype(F32)).astype(BF16)
    return (jnp.concatenate([main, end], axis=0), *sums)


def solution(mesh):
    placed = (
        P(("ctx", "tp"), None),
        P(("ctx", "tp"), None),
        P(None, "tp"),
        P(None, "tp"),
        P(None, "tp"),
    )
    return jax.shard_map(
        shards,
        mesh=mesh,
        in_specs=placed,
        out_specs=(P("ctx", "tp"), P(None, "tp"), P(None, "tp"), P(None, "tp")),
        check_vma=False,
    )
```

```python
import math

import jax
import jax.numpy as jnp
import numpy as np
from jax import lax
from jax.experimental import pallas as pl
from jax.experimental.pallas import tpu as pltpu
from jax.sharding import PartitionSpec as P

F32 = jnp.float32
BF16 = jnp.bfloat16
VMEM_LIMIT = 16 * 1024 * 1024
BLOCK = 1024
BRIEF = pl.CostEstimate(flops=1000, bytes_accessed=1000, transcendentals=0)
LONG = pl.CostEstimate(flops=20_000_000_000, bytes_accessed=100_000_000, transcendentals=0)


STRIP = 16


def strips(rows):
    return [slice(i, i + STRIP) for i in range(0, rows, STRIP)]


def put_halves(x, high_ref, low_ref, rows):
    high = x.astype(BF16)
    high_ref[rows] = high
    low_ref[rows] = (x - high.astype(F32)).astype(BF16)


def stacked_rows(high_ref, low_ref, rows=slice(None)):
    high = high_ref[rows]
    return jnp.concatenate([high, high, low_ref[rows]], axis=0)


def product(matrix, x):
    return jnp.dot(matrix, x, preferred_element_type=F32)


def transforms(extent):
    points = 2 * extent
    angle = np.pi * np.outer(2 * np.arange(extent) + 1, np.arange(points)) / points
    whole = np.concatenate([np.cos(angle), -np.sin(angle)])
    back = whole.T / extent

    def split(matrix, terms=3):
        high = matrix.astype(jnp.bfloat16)
        low = (matrix - high.astype(np.float64)).astype(jnp.bfloat16)
        return np.concatenate([high, low, high][:terms], axis=1)

    return {
        "both": split(whole, 2),
        "short": split(whole[:, :extent]),
        "inverse": split(np.concatenate([-back[extent:], back[:extent]])),
        "around": split(-back[extent - STRIP :]),
    }


def delayed(before, x, by):
    return pltpu.roll(jnp.concatenate([before, x], axis=0), by, 0)[8:]


def advanced(x, after, by):
    both = jnp.concatenate([x, after], axis=0)
    return pltpu.roll(both, both.shape[0] - by, 0)[: x.shape[0]]


def folded(x):
    return sum(x[i : i + 8] for i in range(8, x.shape[0], 8)) + x[:8]


def filtered(u, before, taps):
    value = taps[0] * u
    for j in range(1, len(taps)):
        value = value + taps[j] * delayed(before, u, j)
    return value


def convolved(matrix, spectrum, hs_ref, high_ref, low_ref):
    for at in strips(hs_ref.shape[0] // 2):
        im = slice(at.start + hs_ref.shape[0] // 2, at.stop + hs_ref.shape[0] // 2)
        ur, ui, hr, hi = spectrum[at], spectrum[im], hs_ref[at], hs_ref[im]
        put_halves(ur * hr - ui * hi, high_ref, low_ref, at)
        put_halves(ur * hi + ui * hr, high_ref, low_ref, im)
    return product(matrix, stacked_rows(high_ref, low_ref))


def twice(x):
    return jnp.concatenate([x, x], axis=0)


def signal_kernel(
    u_ref, halo_ref, h_ref, w_ref, both_ref, short_ref, around_ref, us_ref, hs_ref, z_ref, *scratch
):
    high_h, low_h, high_p, low_p, p_ref = scratch
    extent = h_ref.shape[0]
    lead, width = halo_ref.shape
    blocks = us_ref.shape[0]
    for at in strips(extent):
        put_halves(-h_ref[at], high_h, low_h, at)
    hs_ref[...] = product(short_ref[...], stacked_rows(high_h, low_h))
    for b in range(blocks):
        last = u_ref[b * extent : (b + 1) * extent]
        first = halo_ref[lead - extent :] if b == 0 else u_ref[(b - 1) * extent : b * extent]
        us_ref[b] = product(both_ref[...], jnp.concatenate([first, last] * 2, axis=0))
    for b in range(blocks):
        matrix = around_ref[...] if b == 0 else around_ref[STRIP:]
        rows = slice(0 if b == 0 else STRIP + b * extent, STRIP + (b + 1) * extent)
        p_ref[rows] = convolved(matrix, us_ref.at[b], hs_ref, high_p.at[b], low_p.at[b])
    ahead = halo_ref[lead - extent - STRIP : lead - extent].astype(F32)[STRIP - 1 :]
    final = u_ref[extent - STRIP : extent].astype(F32)[STRIP - 1 :]
    mend = h_ref[extent - 1 : extent] * (ahead + final)
    at_second = lax.broadcasted_iota(jnp.int32, (8, width), 0) == 6
    before = p_ref[8:STRIP] + jnp.where(at_second, mend, 0.0)
    w = [w_ref[i : i + 1] for i in range(w_ref.shape[0])]
    for at in strips(z_ref.shape[0]):
        p = p_ref[STRIP + at.start : STRIP + at.stop]
        z_ref[at] = filtered(p, before, w)
        before = p[-8:]


def sums_kernel(
    scale, g_ref, u_ref, halo_ref, h_ref, us_ref, z_ref, gate_ref, w_ref, short_ref, inverse_ref,
    d_ref, dq_ref, sums_ref, *scratch
):
    high_d, low_d, high_c, low_c = scratch
    extent = h_ref.shape[0]
    rows, width = u_ref.shape
    taps = gate_ref.shape[0]
    blocks = rows // extent
    gate = [gate_ref[i : i + 1] for i in range(taps)]
    w = [w_ref[i : i + 1] for i in range(taps)]
    gate_sums = [jnp.zeros((8, width), F32) for _ in range(taps)]
    ahead = halo_ref[halo_ref.shape[0] - STRIP :].astype(F32)
    before = ahead[8:]
    first = halo_ref[halo_ref.shape[0] - extent - STRIP : halo_ref.shape[0] - extent].astype(F32)
    preceding = [first[STRIP - 1 :], ahead[STRIP - 1 :]]
    mend = None
    for at in strips(rows):
        g, u = g_ref[at].astype(F32), u_ref[at].astype(F32)
        late = [u] + [delayed(before, u, i) for i in range(1, taps)]
        before = u[8:]
        q = gate[0] * u
        for i in range(1, taps):
            q = q + gate[i] * late[i]
        dz, dq = g * q, g * z_ref[at]
        dq_ref[at] = dq
        put_halves(dz, high_d, low_d, at)
        gate_sums = [total + folded(dq * x) for total, x in zip(gate_sums, late)]
        if at.start % extent == 0:
            b, start = at.start // extent, dz[:1]
            if b >= 2:
                preceding.append(u_ref[(b - 1) * extent - STRIP : (b - 1) * extent].astype(F32)[STRIP - 1 :])
        if at.stop % extent == 0:
            term = start * (u[STRIP - 1 :] + preceding[b])
            mend = term if mend is None else mend + term
    for b in range(blocks):
        window = slice(b * extent, (b + 1) * extent)
        d_ref[b] = product(short_ref[...], stacked_rows(high_d, low_d, window))
    for at in strips(extent):
        im = slice(extent + at.start, extent + at.stop)
        cr = ci = None
        for b in range(blocks):
            dr, di, ur, ui = d_ref[b, at], d_ref[b, im], us_ref[b, at], us_ref[b, im]
            real, imaginary = dr * ur + di * ui, di * ur - dr * ui
            cr, ci = (real, imaginary) if cr is None else (cr + real, ci + imaginary)
        put_halves(cr, high_c, low_c, at)
        put_halves(ci, high_c, low_c, im)
    lags = product(inverse_ref[: extent + STRIP], stacked_rows(high_c, low_c)) * scale
    at_last = lax.broadcasted_iota(jnp.int32, (8, width), 0) == 1
    after = lags[extent : extent + 8] + jnp.where(at_last, mend * scale, 0.0)
    value_sums = [jnp.zeros((8, width), F32) for _ in range(taps)]
    for row in range(extent - STRIP, -1, -STRIP):
        c = lags[row : row + STRIP]
        early = [c] + [advanced(c, after, i) for i in range(1, taps)]
        after = c[:8]
        total = w[0] * c
        for i in range(1, taps):
            total = total + w[i] * early[i]
        sums_ref[row : row + STRIP] = total
        h = h_ref[row : row + STRIP]
        value_sums = [sums + folded(h * x) for sums, x in zip(value_sums, early)]
    rest = [jnp.sum(x, axis=0, keepdims=True) * scale for x in gate_sums]
    rest += [jnp.sum(x, axis=0, keepdims=True) for x in value_sums]
    spare = sums_ref.shape[0] - extent - 2 * taps
    rest.append(jnp.zeros((spare, width), F32))
    sums_ref[extent:] = jnp.concatenate(rest, axis=0)


def input_kernel(
    lead, d_ref, dq_ref, hs_ref, gate_ref, w_ref, inverse_ref, grad_ref, end_ref, head_ref, *scratch
):
    high_r, low_r, r_ref = scratch
    extent = hs_ref.shape[0] // 2
    rows, width = dq_ref.shape
    taps = gate_ref.shape[0]
    blocks = rows // extent
    for at in strips(extent):
        im = slice(extent + at.start, extent + at.stop)
        hr, hi = hs_ref[at], hs_ref[im]
        for b in range(blocks):
            dr, di = d_ref[b, at], d_ref[b, im]
            put_halves(dr * hr + di * hi, high_r.at[b], low_r.at[b], at)
            put_halves(di * hr - dr * hi, high_r.at[b], low_r.at[b], im)
    for b in range(blocks):
        r_ref[b] = product(inverse_ref[...], stacked_rows(high_r.at[b], low_r.at[b]))
    w = [-w_ref[i : i + 1] for i in range(taps)]
    gate = [gate_ref[i : i + 1] for i in range(taps)]
    nothing = jnp.zeros((STRIP, width), F32)
    after_r = after_dq = nothing[:8]
    for row in range(rows - STRIP, -lead - 1, -STRIP):
        block, at = (row + extent) // extent, (row + extent) % extent
        if row < -extent:
            r = nothing
        elif block == 0:
            r = r_ref[0, at : at + STRIP]
        elif block == blocks:
            r = r_ref[blocks - 1, extent + at : extent + at + STRIP]
        else:
            r = r_ref[block - 1, extent + at : extent + at + STRIP] + r_ref[block, at : at + STRIP]
        total = w[0] * r
        for i in range(1, taps):
            total = total + w[i] * advanced(r, after_r, i)
        after_r = r[:8]
        if row >= -STRIP:
            dq = dq_ref[row : row + STRIP] if row >= 0 else nothing
            if row >= 0:
                total = total + gate[0] * dq
            for i in range(1, taps):
                total = total + gate[i] * advanced(dq, after_dq, i)
            after_dq = dq[:8]
        if row < 0:
            head_ref[lead + row : lead + row + STRIP] = total.astype(BF16)
        elif row < rows - lead:
            grad_ref[row : row + STRIP] = total.astype(BF16)
        else:
            end_ref[row - rows + lead : row - rows + lead + STRIP] = total


IN_VMEM = pl.BlockSpec(memory_space=pltpu.VMEM)
IN_SMEM = pl.BlockSpec(memory_space=pltpu.SMEM)
ANYWHERE = pl.BlockSpec(memory_space=pl.ANY)


def place_of(me_ref, k, pieces, piece):
    return pl.ds(pl.multiple_of(lax.rem(me_ref[0] + (pieces - k), pieces) * piece, piece), piece)


def call(name, body, inputs, constants, outs, scratch, block, cost, me, pieces=(), kept_outs=(), at_end=None):
    moved = [isinstance(x, list) for x in inputs]
    arrays = [x[0] if isinstance(x, list) else x for x in inputs]
    width = arrays[0].shape[-1]
    blocks = width // block
    last_outs = () if at_end is None else at_end[0]
    n_pieces, n_in, n_const = len(pieces), len(arrays), len(constants)
    n_out = len(outs) + len(last_outs)
    held = [x for x, move in zip(arrays, moved) if move] + list(constants) + list(kept_outs)
    if pieces:
        held.append(jax.ShapeDtypeStruct((n_pieces * pieces[0].shape[0], width), pieces[0].dtype))

    def kernel(*refs):
        me_ref, piece_refs, refs = refs[0], refs[1 : 1 + n_pieces], refs[1 + n_pieces :]
        given, refs = refs[: n_in + n_const], refs[n_in + n_const :]
        results, refs = refs[:n_out], refs[n_out:]
        temporary, kept, sems, const_sems = refs[: len(scratch)], list(refs[len(scratch) : -2]), *refs[-2:]
        ins, sources = [], []
        for ref, move in zip(given, moved):
            ins.append(kept.pop(0) if move else ref)
            if move:
                sources.append((ref, ins[-1]))
        whole = [kept.pop(0) for _ in range(n_const)]
        stay = [kept.pop(0) for _ in kept_outs]
        if pieces:
            ins.insert(0, kept.pop(0))
            sources += [
                (ref, ins[0].at[place_of(me_ref, k, n_pieces, ref.shape[0])]) for k, ref in enumerate(piece_refs)
            ]

        def cut(ref, j):
            place = pl.ds(pl.multiple_of(j * block, block), block)
            return ref.at[(slice(None),) * (len(ref.shape) - 1) + (place,)]

        def copies(j):
            return [pltpu.make_async_copy(cut(a, j), cut(b, j), sems.at[i, j]) for i, (a, b) in enumerate(sources)]

        constant_copies = [
            pltpu.make_async_copy(a, b, const_sems.at[i]) for i, (a, b) in enumerate(zip(given[n_in:], whole))
        ]
        for copy in constant_copies:
            copy.start()
        for j in range(blocks):
            for copy in copies(j):
                copy.start()
        for copy in constant_copies:
            copy.wait()

        def one(j):
            for copy in copies(j):
                copy.wait()
            shown = list(results[: len(outs)]) + stay
            body(*[cut(x, j) for x in ins], *whole, *[cut(x, j) for x in shown], *temporary)

        pl.loop(0, blocks)(one)
        if at_end is not None:
            at_end[1](me_ref, stay, results[len(outs) :])

    return pl.pallas_call(
        kernel,
        in_specs=[IN_SMEM]
        + [ANYWHERE] * n_pieces
        + [ANYWHERE if move else IN_VMEM for move in moved]
        + [ANYWHERE] * n_const,
        out_specs=[IN_VMEM] * n_out,
        scratch_shapes=[pltpu.VMEM(shape, dtype) for shape, dtype in scratch]
        + [pltpu.VMEM(x.shape, x.dtype) for x in held]
        + [
            pltpu.SemaphoreType.DMA((n_pieces + sum(moved) + 1, blocks)),
            pltpu.SemaphoreType.DMA((n_const,)),
        ],
        out_shape=[*outs, *last_outs],
        compiler_params=pltpu.CompilerParams(vmem_limit_bytes=VMEM_LIMIT),
        cost_estimate=cost,
        name=name,
    )(me, *pieces, *arrays, *constants)


def tail_step(pieces, me, lead):
    piece, width = pieces[0].shape
    rows = piece * len(pieces)

    def kernel(me_ref, *refs):
        tail_ref, held, sems, sem = refs[len(pieces) :]
        copies = [
            pltpu.make_async_copy(ref, held.at[place_of(me_ref, k, len(pieces), piece)], sems.at[k])
            for k, ref in enumerate(refs[: len(pieces)])
        ]
        for copy in copies:
            copy.start()
        for copy in copies:
            copy.wait()
        out = pltpu.make_async_copy(held.at[pl.ds(rows - lead, lead), :], tail_ref, sem)
        out.start()
        out.wait()

    return pl.pallas_call(
        kernel,
        in_specs=[IN_SMEM] + [ANYWHERE] * len(pieces),
        out_specs=ANYWHERE,
        scratch_shapes=[
            pltpu.VMEM((rows, width), BF16),
            pltpu.SemaphoreType.DMA((len(pieces),)),
            pltpu.SemaphoreType.DMA,
        ],
        out_shape=jax.ShapeDtypeStruct((lead, width), BF16),
        compiler_params=pltpu.CompilerParams(vmem_limit_bytes=VMEM_LIMIT),
        cost_estimate=BRIEF,
        name="tail_step",
    )(me, *pieces)


def signal_step(u_pieces, me, halo, h, w, matrices, block):
    width = h.shape[1]
    rows, extent = u_pieces[0].shape[0] * len(u_pieces), h.shape[0]
    blocks = rows // extent
    outs = [
        jax.ShapeDtypeStruct((blocks, 2 * extent, width), F32),
        jax.ShapeDtypeStruct((2 * extent, width), F32),
        jax.ShapeDtypeStruct((rows, width), F32),
        jax.ShapeDtypeStruct((rows, width), BF16),
    ]
    scratch = [((extent, block), BF16)] * 2 + [((blocks, 2 * extent, block), BF16)] * 2
    scratch += [((STRIP + rows, block), F32)]
    constants = [matrices[name] for name in ("both", "short", "around")]

    def body(u_ref, *refs):
        refs[9][...] = u_ref[...]
        signal_kernel(u_ref, *refs[:9], *refs[10:])

    return call(
        "signal_step", body, [[halo], [h], [w]], constants, outs, scratch, block, BRIEF, me, u_pieces
    )


def gradient_step(g_pieces, me, u, halo, h, us, hs, z, gate, w, matrices, scale, block, shares):
    rows, width = u.shape
    extent, taps, lead = h.shape[0], gate.shape[0], halo.shape[0]
    blocks = rows // extent
    count, part = extent + -(-2 * taps // 16) * 16, width // shares
    outs = [
        jax.ShapeDtypeStruct((rows - lead, width), BF16),
        jax.ShapeDtypeStruct((lead, width), F32),
        jax.ShapeDtypeStruct((lead, width), BF16),
    ]
    sums = [jax.ShapeDtypeStruct((count, width), F32)]
    spectra = (blocks, 2 * extent, block)
    scratch = [(spectra, F32), ((rows, block), F32)]
    scratch += [((rows, block), BF16)] * 2 + [((2 * extent, block), BF16)] * 2
    scratch += [(spectra, BF16)] * 2 + [(spectra, F32)]
    ends = [jax.ShapeDtypeStruct((count, part), BF16 if k else F32) for k in range(shares)]

    def body(g, u, halo, h, us, hs, z, gate, w, short, inverse, grad, end, head, sums, d, dq, *temporary):
        sums_kernel(scale, g, u, halo, h, us, z, gate, w, short, inverse, d, dq, sums, *temporary[:4])
        input_kernel(lead, d, dq, hs, gate, w, inverse, grad, end, head, *temporary[4:])

    def share(me_ref, kept, refs):
        for k, ref in enumerate(refs):
            start = pl.multiple_of((me_ref[1] ^ k) * part, part) if shares > 1 else 0
            ref[...] = kept[0][:, pl.ds(start, part)].astype(ref.dtype)

    main, end, head, *terms = call(
        "gradient_step", body, [u, [halo], [h], us, hs, z, [gate], [w]],
        [matrices[name] for name in ("short", "inverse")], outs, scratch, block, LONG, me, g_pieces, sums,
        (ends, share),
    )
    return main, end, head, terms


def slices(x, axis, start, part):
    count = lax.axis_size(axis)
    me = lax.axis_index(axis)
    width = x.shape[1] // count
    return [
        lax.dynamic_slice_in_dim(x, lax.rem(me + k, count) * width + start, part, axis=1)
        for k in range(count)
    ]


def exchange(pieces, axis):
    count = lax.axis_size(axis)
    got = [pieces[0]] + [None] * (count - 1)
    for k in sorted(range(1, count), key=lambda k: abs(2 * k - count)):
        got[k] = lax.ppermute(pieces[k], axis, [(i, (i + k) % count) for i in range(count)])
    return got


def shifted(x, axis, by):
    count = lax.axis_size(axis)
    pairs = [(i, i + by) for i in range(count) if 0 <= i + by < count]
    return lax.ppermute(x, axis, pairs)


def at_once(exchange_of, x, axis):
    return lax.cond(lax.axis_index(axis) >= 0, exchange_of, jnp.zeros_like, x)


def partner(x, axis, bit):
    count = lax.axis_size(axis)
    return lax.ppermute(x, axis, [(i, i ^ bit) for i in range(count)])


def summed(x, axis):
    total, bit, count = x + partner(x, axis, 1), 2, lax.axis_size(axis)
    while bit < count:
        short = total.astype(BF16)
        total = short.astype(F32) + partner(short, axis, bit).astype(F32)
        bit *= 2
    return total


def finish_step(terms, me, sizes):
    part, shares = terms[0].shape[1], len(terms)
    width = part * shares

    def kernel(me_ref, *refs):
        terms, outs, held, sems = refs[:shares], refs[shares : shares + len(sizes)], refs[shares + len(sizes) : -1], refs[-1]
        copies = []
        for k, term in enumerate(terms):
            place = pl.ds(pl.multiple_of((me_ref[1] ^ k) * part, part), part)
            x, row = term[...].astype(F32), 0
            for i, (size, out, ref) in enumerate(zip(sizes, outs, held)):
                ref[:, place] = x[row : row + size]
                row += size
                copies.append(pltpu.make_async_copy(ref.at[:, place], out.at[:, place], sems.at[i, k]))
                copies[-1].start()
        for copy in copies:
            copy.wait()

    return pl.pallas_call(
        kernel,
        in_specs=[IN_SMEM] + [IN_VMEM] * shares,
        out_specs=[ANYWHERE] * len(sizes),
        scratch_shapes=[pltpu.VMEM((size, width), F32) for size in sizes]
        + [pltpu.SemaphoreType.DMA((len(sizes), shares))],
        out_shape=[jax.ShapeDtypeStruct((size, width), F32) for size in sizes],
        compiler_params=pltpu.CompilerParams(vmem_limit_bytes=VMEM_LIMIT),
        cost_estimate=BRIEF,
        name="finish_step",
    )(me, *terms)


def shards(out_grad, saved_input, explicit_filter_weights, gate_taps, value_featurizer_weights):
    extent, width = explicit_filter_weights.shape
    taps = gate_taps.shape[0]
    me = jnp.stack([lax.axis_index("tp"), lax.axis_index("ctx") // 2]).astype(jnp.int32)
    rows = out_grad.shape[0] * lax.axis_size("tp")
    lead = -(-(extent + taps - 2) // 16) * 16
    block = min(BLOCK, width)
    matrices = {name: jnp.asarray(m) for name, m in transforms(extent).items()}
    scale = 1.0 / math.sqrt(rows * lax.axis_size("ctx"))
    h, gate, w = explicit_filter_weights, gate_taps, value_featurizer_weights
    u_pieces = exchange(slices(saved_input, "tp", 0, width), "tp")
    g_slices = slices(out_grad, "tp", 0, width)
    u_pieces, g_slices = lax.optimization_barrier((u_pieces, g_slices))
    g_pieces = exchange(g_slices, "tp")
    tail = tail_step(u_pieces, me, lead)
    halo = at_once(lambda x: shifted(x, "ctx", 1), tail, "ctx")
    us, hs, z, u = signal_step(u_pieces, me, halo, h, w, matrices, block)
    chips = lax.axis_size("ctx") // 2
    shares = chips if chips == 4 and width % (128 * chips) == 0 else 1
    main, end, head, terms = gradient_step(
        g_pieces, me, u, halo, h, us, hs, z, gate, w, matrices, scale, block, shares
    )
    sizes = (extent, taps, taps)
    if shares > 1:
        for k in range(shares - 1, 0, -1):
            terms[k] = partner(terms[k], "ctx", 2 * k).astype(F32)
        incoming = shifted(head, "ctx", -1)
        while len(terms) > 1:
            terms = [a + b for a, b in zip(terms[::2], terms[1::2])]
        total = terms[0] + partner(terms[0], "ctx", 1)
        total, incoming = lax.optimization_barrier((total, incoming))
        total = total.astype(BF16)
        terms = [total] + [partner(total, "ctx", 2 * k) for k in range(1, shares)]
        sums = finish_step(terms, me, sizes)
    else:
        incoming = shifted(head, "ctx", -1)
        total = summed(terms[0], "ctx")
        ends = np.cumsum(sizes)
        sums = [total[stop - size : stop] for size, stop in zip(sizes, ends)]
    end = (end + incoming.astype(F32)).astype(BF16)
    return (jnp.concatenate([main, end], axis=0), *sums)


def solution(mesh):
    placed = (
        P(("ctx", "tp"), None),
        P(("ctx", "tp"), None),
        P(None, "tp"),
        P(None, "tp"),
        P(None, "tp"),
    )
    return jax.shard_map(
        shards,
        mesh=mesh,
        in_specs=placed,
        out_specs=(P("ctx", "tp"), P(None, "tp"), P(None, "tp"), P(None, "tp")),
        check_vma=False,
    )
```
